128 devices in a mesh: dp: 32 (over y, x, core), row: 2 (over z_hi), col: 2 (over z_lo).
Axes of the slice: x: 4, y: 4, z: 4 (z_hi: 2, z_lo: 2; z = z_hi * 2 + z_lo), core: 2. Of those that a mesh axis runs over, the one named last changes fastest.
Arguments:
- block_in: bfloat16 [16384, 768], P(('dp', 'row'), 'col'), may hold values from -6 to 6
- out_grad: float32 [16384, 768], P(('dp', 'row'), 'col'), may hold values from -6 to 6
- seq_lengths: int32 [32, 4], P('dp'), may hold values from 1 to 384, 512 in all within a row
- weight_qkv: float32 [768, 3, 2, 384], P('col', None, 'row', 'dp'), may hold values from -0.21875 to 0.21875
- first_qkv: float32 [768, 3, 2, 384], P('col', None, 'row', 'dp'), may hold values from -64 to 64
- second_qkv: float32 [768, 3, 2, 384], P('col', None, 'row', 'dp'), may hold values from 8.192 to 32.768
- weight_out: float32 [768, 2, 384], P('row', 'col', 'dp'), may hold values from -1.25 to 1.25
- first_out: float32 [768, 2, 384], P('row', 'col', 'dp'), may hold values from -16 to 16
- second_out: float32 [768, 2, 384], P('row', 'col', 'dp'), may hold values from 0.65536 to 2.62144
- weight_up: float32 [768, 2, 1536], P('col', 'row', 'dp'), may hold values from -0.21875 to 0.21875
- first_up: float32 [768, 2, 1536], P('col', 'row', 'dp'), may hold values from -24 to 24
- second_up: float32 [768, 2, 1536], P('col', 'row', 'dp'), may hold values from 1.47456 to 5.89824
- weight_down: float32 [3072, 2, 384], P('row', 'col', 'dp'), may hold values from -0.109375 to 0.109375
- first_down: float32 [3072, 2, 384], P('row', 'col', 'dp'), may hold values from -48 to 48
- second_down: float32 [3072, 2, 384], P('row', 'col', 'dp'), may hold values from 5.89824 to 23.59296
- col_params: float32 [6, 2, 384], P(None, 'col', 'dp'), as said below
- first_col: float32 [6, 2, 384], P(None, 'col', 'dp'), may hold values from -80 to 80
- second_col: float32 [6, 2, 384], P(None, 'col', 'dp'), may hold values from 16.384 to 65.536
- bias_qv: float32 [2, 2, 384], P(None, 'row', 'dp'), may hold values from -1.75 to 1.75
- first_qv: float32 [2, 2, 384], P(None, 'row', 'dp'), may hold values from -64 to 64
- second_qv: float32 [2, 2, 384], P(None, 'row', 'dp'), may hold values from 8.192 to 32.768
- bias_up: float32 [2, 1536], P('row', 'dp'), may hold values from -1.75 to 1.75
- first_bup: float32 [2, 1536], P('row', 'dp'), may hold values from -24 to 24
- second_bup: float32 [2, 1536], P('row', 'dp'), may hold values from 1.47456 to 5.89824
Outputs:
- block_out: float32 [16384, 768], P(('dp', 'row'), 'col')
- grad_in: float32 [16384, 768], P(('dp', 'row'), 'col')
- grad_qkv: float32 [768, 3, 2, 384], P('col', None, 'row', 'dp')
- moment_qkv: float32 [768, 3, 2, 384], P('col', None, 'row', 'dp')
- new_qkv: float32 [768, 3, 2, 384], P('col', None, 'row', 'dp')
- grad_outproj: float32 [768, 2, 384], P('row', 'col', 'dp')
- moment_outproj: float32 [768, 2, 384], P('row', 'col', 'dp')
- new_outproj: float32 [768, 2, 384], P('row', 'col', 'dp')
- grad_upproj: float32 [768, 2, 1536], P('col', 'row', 'dp')
- moment_upproj: float32 [768, 2, 1536], P('col', 'row', 'dp')
- new_upproj: float32 [768, 2, 1536], P('col', 'row', 'dp')
- grad_downproj: float32 [3072, 2, 384], P('row', 'col', 'dp')
- moment_downproj: float32 [3072, 2, 384], P('row', 'col', 'dp')
- new_downproj: float32 [3072, 2, 384], P('row', 'col', 'dp')
- grad_colvec: float32 [6, 2, 384], P(None, 'col', 'dp')
- moment_colvec: float32 [6, 2, 384], P(None, 'col', 'dp')
- new_colvec: float32 [6, 2, 384], P(None, 'col', 'dp')
- grad_qvbias: float32 [2, 2, 384], P(None, 'row', 'dp')
- moment_qvbias: float32 [2, 2, 384], P(None, 'row', 'dp')
- new_qvbias: float32 [2, 2, 384], P(None, 'row', 'dp')
- grad_upbias: float32 [2, 1536], P('row', 'dp')
- moment_upbias: float32 [2, 1536], P('row', 'dp')
- new_upbias: float32 [2, 1536], P('row', 'dp')
The draws below stay inside these ranges and needn't reach their ends.
Inputs may be any that keep to these rules, and one draw needn't show every extreme that they name: `seq_lengths`: each row sums to 512; in every row the longest sequence has exactly 384 tokens. `col_params`: rows 0 and 2 (the gains) lie in 0.6 to 1.4, the other rows are normal with deviation 0.3.
All inputs are finite; a program needn't handle non-finite values.
Results may differ from the reference program's by a relative error of at most 0.012.
The reference program's roundings to bfloat16 on the way count: a program that leaves them out, or rounds other values in their place, can miss the bound.
Values may be sent and summed in bfloat16 or wider, within the bound.
No kernel may reach another device: no remote copies, remote signals or barrier semaphores. Data moves between devices by JAX's collectives and lax.ppermute only.
A program may use at most 128 MiB of HBM per device.

```python
import math
import jax
import jax.numpy as jnp
import numpy as np
from jax import lax

H = 12
HD = 64
FF = 3072
D = 768
SEQS = 4
STEP = 10
GROUP_TOK = 512
TOKENS = 16384
MAXLEN = 384
DC = 384
DR = 384
FR = 1536
N_DP = 32
N_ROW = 2
N_COL = 2


def draw_col_params(key, part):
    key = jax.random.fold_in(key, 11)
    key_gain, key_shift = jax.random.split(key)
    gains = jax.random.uniform(key_gain, (6, N_COL, DC), jnp.float32, 0.6, 1.4)
    shifts = 0.3 * jax.random.normal(key_shift, (6, N_COL, DC), jnp.float32)
    chosen = (jnp.arange(6) % 2 == 0) & (jnp.arange(6) < 4)
    return jnp.where(chosen[:, None, None], gains, shifts)


def block_levels(key, shape, cuts, smallest, largest):
    def one(position, parts):
        draws = jax.random.uniform(jax.random.fold_in(jax.random.fold_in(key, 6), position), (parts,), jnp.float32, smallest / len(cuts), largest / len(cuts))
        return jnp.repeat(jnp.exp(draws), shape[position] // parts).reshape((-1,) + (1,) * (len(shape) - position - 1))

    loudness = one(*cuts[0])
    for cut in cuts[1:]:
        loudness = loudness * one(*cut)
    return loudness


def split_up(number_of, total, reach, skew):
    loads = [(1 << 20) // math.isqrt(grade ** skew) + 1 for grade in range(2, number_of + 1)]
    spare, counts = total - reach - (number_of - 1), [1] * (number_of - 1)
    while spare > 0:
        candidates = [i for i in range(number_of - 1) if counts[i] < reach]
        whole, left = sum([loads[i] for i in candidates]), spare
        for i in candidates:
            addition = min(reach - counts[i], max(1, left * loads[i] // whole), spare)
            counts[i] = counts[i] + addition
            spare = spare - addition
    return np.array([reach] + counts)


def uneven_parts(key, number_of, total, reach, skew):
    if number_of == 2:
        one = jax.random.randint(key, (), max(1, total - reach), min(reach, total - 1) + 1)
        return jnp.stack([one, total - one])
    sizes = jnp.asarray(split_up(number_of, total, reach, skew), jnp.int32)
    couples = (number_of - 1) // 2
    giver, receiver = sizes[1:1 + 2 * couples:2], sizes[2:2 + 2 * couples:2]
    margin = jnp.minimum(giver - 1, reach - receiver)
    moved = jax.random.randint(jax.random.fold_in(key, 1), (couples,), 0, 1 << 20) % (margin + 1)
    sizes = sizes.at[1:1 + 2 * couples:2].set(giver - moved).at[2:2 + 2 * couples:2].set(receiver + moved)
    return sizes[jax.random.permutation(jax.random.fold_in(key, 2), number_of)]


def noise(key, dims, scale, bound, cuts=(), held_as=jnp.bfloat16):
    entries = jax.random.normal(key, dims, jnp.float32) * scale
    if len(cuts) > 0:
        entries = block_levels(key, dims, cuts, -0.22, 0.18) * entries
    return jnp.clip(entries, min=-bound, max=bound).astype(held_as)


def setup_inputs(seed: int = 0) -> dict:
    keys = jax.random.split(jax.random.key(seed), 25)
    block_in = noise(keys[0], (TOKENS, D), 1.0, 6.0, ((0, 64), (1, 2)))
    out_grad = noise(keys[1], (TOKENS, D), 1.0, 6.0, ((0, 64), (1, 2)), jnp.float32)
    seq_lengths = jax.vmap(lambda own: uneven_parts(own, SEQS, GROUP_TOK, MAXLEN, 2))(jax.random.split(keys[2], N_DP)).reshape((N_DP, SEQS)).astype(jnp.int32)
    weight_qkv = noise(keys[3], (D, 3, N_ROW, DR), D ** -0.5, 0.21875, ((0, 2), (2, 2), (3, 32)), jnp.float32)
    first_qkv = noise(keys[4], (D, 3, N_ROW, DR), (0.08 * TOKENS ** 0.5), 64.0, ((0, 2), (2, 2), (3, 32)), jnp.float32)
    second_qkv = jnp.clip(jnp.exp(math.log(32.768) - 1.3862944 * jax.random.uniform(keys[5], (D, 3, N_ROW, DR), jnp.float32) ** block_levels(keys[5], (D, 3, N_ROW, DR), ((0, 2), (2, 2), (3, 32)), -0.2, 0.2)), 8.192, 32.768)
    weight_out = noise(keys[6], (D, N_COL, DC), (D * 16 // GROUP_TOK) ** -0.5, 1.25, ((0, 2), (1, 2), (2, 32)), jnp.float32)
    first_out = noise(keys[7], (D, N_COL, DC), (0.022 * TOKENS ** 0.5), 16.0, ((0, 2), (1, 2), (2, 32)), jnp.float32)
    second_out = jnp.clip(jnp.exp(math.log(2.62144) - 1.3862944 * jax.random.uniform(keys[8], (D, N_COL, DC), jnp.float32) ** block_levels(keys[8], (D, N_COL, DC), ((0, 2), (1, 2), (2, 32)), -0.2, 0.2)), 0.65536, 2.62144)
    weight_up = noise(keys[9], (D, N_ROW, FR), D ** -0.5, 0.21875, ((0, 2), (1, 2), (2, 32)), jnp.float32)
    first_up = noise(keys[10], (D, N_ROW, FR), (0.033 * TOKENS ** 0.5), 24.0, ((0, 2), (1, 2), (2, 32)), jnp.float32)
    second_up = jnp.clip(jnp.exp(math.log(5.89824) - 1.3862944 * jax.random.uniform(keys[11], (D, N_ROW, FR), jnp.float32) ** block_levels(keys[11], (D, N_ROW, FR), ((0, 2), (1, 2), (2, 32)), -0.2, 0.2)), 1.47456, 5.89824)
    weight_down = noise(keys[12], (FF, N_COL, DC), FF ** -0.5, 0.109375, ((0, 2), (1, 2), (2, 32)), jnp.float32)
    first_down = noise(keys[13], (FF, N_COL, DC), (0.066 * TOKENS ** 0.5), 48.0, ((0, 2), (1, 2), (2, 32)), jnp.float32)
    second_down = jnp.clip(jnp.exp(math.log(23.59296) - 1.3862944 * jax.random.uniform(keys[14], (FF, N_COL, DC), jnp.float32) ** block_levels(keys[14], (FF, N_COL, DC), ((0, 2), (1, 2), (2, 32)), -0.2, 0.2)), 5.89824, 23.59296)
    col_params = draw_col_params(jax.random.fold_in(keys[24], 71), 0)
    first_col = noise(keys[16], (6, N_COL, DC), (0.11 * TOKENS ** 0.5), 80.0, ((1, 2), (2, 32)), jnp.float32)
    second_col = jnp.clip(jnp.exp(math.log(65.536) - 1.3862944 * jax.random.uniform(keys[17], (6, N_COL, DC), jnp.float32) ** block_levels(keys[17], (6, N_COL, DC), ((1, 2), (2, 32)), -0.2, 0.2)), 16.384, 65.536)
    bias_qv = noise(keys[18], (2, N_ROW, DR), 0.3, 1.75, ((1, 2), (2, 32)), jnp.float32)
    first_qv = noise(keys[19], (2, N_ROW, DR), (0.08 * TOKENS ** 0.5), 64.0, ((1, 2), (2, 32)), jnp.float32)
    second_qv = jnp.clip(jnp.exp(math.log(32.768) - 1.3862944 * jax.random.uniform(keys[20], (2, N_ROW, DR), jnp.float32) ** block_levels(keys[20], (2, N_ROW, DR), ((1, 2), (2, 32)), -0.2, 0.2)), 8.192, 32.768)
    bias_up = noise(keys[21], (N_ROW, FR), 0.3, 1.75, ((0, 2), (1, 32)), jnp.float32)
    first_bup = noise(keys[22], (N_ROW, FR), (0.033 * TOKENS ** 0.5), 24.0, ((0, 2), (1, 32)), jnp.float32)
    second_bup = jnp.clip(jnp.exp(math.log(5.89824) - 1.3862944 * jax.random.uniform(keys[23], (N_ROW, FR), jnp.float32) ** block_levels(keys[23], (N_ROW, FR), ((0, 2), (1, 32)), -0.2, 0.2)), 1.47456, 5.89824)
    return dict(block_in=block_in, out_grad=out_grad, seq_lengths=seq_lengths, weight_qkv=weight_qkv, first_qkv=first_qkv, second_qkv=second_qkv, weight_out=weight_out, first_out=first_out, second_out=second_out, weight_up=weight_up, first_up=first_up, second_up=second_up, weight_down=weight_down, first_down=first_down, second_down=second_down, col_params=col_params, first_col=first_col, second_col=second_col, bias_qv=bias_qv, first_qv=first_qv, second_qv=second_qv, bias_up=bias_up, first_bup=first_bup, second_bup=second_bup)


@jax.custom_vjp
def low(v):
    return lax.optimization_barrier(v.astype(jnp.bfloat16)).astype(jnp.float32)

@jax.custom_vjp
def low_back(v):
    return v

def low_keep(v):
    return (low(v), None)

def low_pass(kept, grad):
    return (grad,)

def back_keep(v):
    return (v, None)

def back_low(kept, grad):
    return (low(grad),)
low.defvjp(low_keep, low_pass)
low_back.defvjp(back_keep, back_low)
norm_eps = 1e-05
beta_one = 0.9
beta_two = 0.999
adam_eps = 1e-08
decay_rate = 0.1
neg_large = -1e+30
highest = lax.Precision.HIGHEST
step_rates = (0.25, 0.4, 0.25, 0.25, 0.3, 0.3, 0.3)

def layer_norm(values, gain, shift):
    mean = lax.optimization_barrier(jnp.mean(values, axis=-1, keepdims=True))
    centered = values - mean
    spread = lax.optimization_barrier(jnp.mean(centered * centered, axis=-1, keepdims=True))
    return centered * lax.rsqrt(spread + norm_eps) * gain + shift

def group_forward(params, rows_in, allowed):
    weight_qkv, weight_out, weight_up, weight_down, col_vec, bias_qv, bias_up = params
    tokens = rows_in.shape[0]
    normed = low(layer_norm(rows_in, col_vec[0], col_vec[1]))
    bias_all = jnp.stack([bias_qv[0], jnp.zeros_like(bias_qv[0]), bias_qv[1]])
    packed = jnp.einsum('td,djf->tjf', normed, weight_qkv, precision=highest) + bias_all
    packed = low_back(low(packed))
    heads = packed.reshape(tokens, 3, H, HD).transpose(1, 2, 0, 3)

    def one_head(triple):
        queries, keys_in, values_in = triple
        raw = jnp.dot(queries, keys_in.T, precision=highest) * HD ** (-0.5)
        scores = jnp.where(allowed, low_back(raw), neg_large)
        shifted = scores - lax.optimization_barrier(jnp.max(scores, axis=-1, keepdims=True))
        weights = jnp.exp(shifted)
        probs = weights / lax.optimization_barrier(jnp.sum(weights, axis=-1, keepdims=True))
        return jnp.dot(low(probs), values_in, precision=highest)
    mixed = lax.map(jax.checkpoint(one_head), (heads[0], heads[1], heads[2]))
    attended = low_back(low(mixed.transpose(1, 0, 2).reshape(tokens, H * HD)))
    middle = rows_in + low_back(jnp.dot(attended, weight_out, precision=highest)) + col_vec[4]
    normed_two = low(layer_norm(middle, col_vec[2], col_vec[3]))
    hidden = low_back(jnp.dot(normed_two, weight_up, precision=highest) + bias_up)
    active = low(jax.nn.gelu(hidden))
    return middle + low_back(jnp.dot(active, weight_down, precision=highest)) + col_vec[5]

def adam_update(master, first_old, second_old, gradient, step_rate):
    first_new = beta_one * first_old + (1.0 - beta_one) * gradient
    second_new = beta_two * second_old + (1.0 - beta_two) * gradient * gradient
    ratio = first_new / (1.0 - beta_one ** STEP) / (jnp.sqrt(second_new / (1.0 - beta_two ** STEP)) + adam_eps)
    return (second_new, master - step_rate * (ratio + decay_rate * master))

def reference(block_in, out_grad, seq_lengths, weight_qkv, first_qkv, second_qkv, weight_out, first_out, second_out, weight_up, first_up, second_up, weight_down, first_down, second_down, col_params, first_col, second_col, bias_qv, first_qv, second_qv, bias_up, first_bup, second_bup):
    masters = (weight_qkv, weight_out, weight_up, weight_down, col_params, bias_qv, bias_up)
    firsts = (first_qkv, first_out, first_up, first_down, first_col, first_qv, first_bup)
    seconds = (second_qkv, second_out, second_up, second_down, second_col, second_qv, second_bup)
    params = (low(weight_qkv.reshape(D, 3, D)), low(weight_out.reshape(D, D)), low(weight_up.reshape(D, FF)), low(weight_down.reshape(FF, D)), low(col_params.reshape(6, D)), low(bias_qv.reshape(2, D)), low(bias_up.reshape(FF)))

    def one_group(totals, pieces):
        rows_in, cotangent, lengths = pieces
        ends = jnp.cumsum(lengths).astype(jnp.int32)
        places = jnp.arange(GROUP_TOK, dtype=jnp.int32)
        segment = lax.optimization_barrier(jnp.sum((places[:, None] >= ends[None, :]).astype(jnp.int32), axis=1))
        allowed = (segment[:, None] == segment[None, :]) & (places[None, :] <= places[:, None])

        def forward(weights, inputs_f):
            return group_forward(weights, inputs_f, allowed)
        result, pullback = jax.vjp(forward, params, rows_in.astype(jnp.float32))
        grads, grad_rows = pullback(cotangent)
        return (jax.tree.map(jnp.add, totals, grads), (result, grad_rows))
    zeros = jax.tree.map(jnp.zeros_like, params)
    totals, outputs = lax.scan(one_group, zeros, (block_in.reshape(N_DP, GROUP_TOK, D), out_grad.reshape(N_DP, GROUP_TOK, D), seq_lengths))
    results = []
    for master, first_old, second_old, total, step_rate in zip(masters, firsts, seconds, totals, step_rates):
        gradient = total.reshape(master.shape)
        second_new, updated = adam_update(master, first_old, second_old, gradient, step_rate)
        results.append((gradient, second_new, updated))
    return (outputs[0].reshape(TOKENS, D), outputs[1].reshape(TOKENS, D), results[0][0], results[0][1], results[0][2], results[1][0], results[1][1], results[1][2], results[2][0], results[2][1], results[2][2], results[3][0], results[3][1], results[3][2], results[4][0], results[4][1], results[4][2], results[5][0], results[5][1], results[5][2], results[6][0], results[6][1], results[6][2])
```

```python
import functools

import jax
import jax.numpy as jnp
import numpy as np
from jax import lax
from jax.experimental import pallas as pl
from jax.experimental.pallas import tpu as pltpu
from jax.sharding import Mesh
from jax.sharding import PartitionSpec as P

HD = 64
D = 768
HALF = 384
FF = 3072
TOK = 512
N_DP = 32
STEP = 10

norm_eps = 1e-05
beta_one = 0.9
beta_two = 0.999
adam_eps = 1e-08
decay_rate = 0.1
neg_large = -1e30
step_rates = (0.25, 0.4, 0.25, 0.25, 0.3, 0.3, 0.3)

DP = ("y", "x", "core")
ALL = ("y", "x", "core", "row", "col")
bf16 = jnp.bfloat16
f32 = jnp.float32
VMEM = pltpu.VMEM


def swap_matrix():
    places = np.arange(192).reshape(4, 4, 12).transpose(1, 0, 2).reshape(192)
    return jnp.asarray(np.eye(192, dtype=np.float32)[places], dtype=bf16)


def dot_nn(a, b):
    return lax.dot_general(a, b, (((1,), (0,)), ((), ())), preferred_element_type=f32)


def dot_nt(a, b):
    return lax.dot_general(a, b, (((1,), (1,)), ((), ())), preferred_element_type=f32)


def dot_tn(a, b):
    return lax.dot_general(a, b, (((0,), (0,)), ((), ())), preferred_element_type=f32)


def unpack_kernel(swap_ref, got_ref, qkv_ref, out_ref, up_ref, down_ref):
    swap = swap_ref[...]
    for g in range(8):
        four = [got_ref[4 * g + i, 0] for i in range(4)]
        attn = jnp.concatenate([piece[0:48] for piece in four], axis=0)
        attn = dot_nn(swap, attn).astype(bf16)
        for j in range(3):
            qkv_ref[j, 48 * g : 48 * g + 48, :] = attn[48 * j : 48 * j + 48]
        out_ref[48 * g : 48 * g + 48, :] = attn[144:192]
        for i in range(4):
            first = 48 * (4 * g + i)
            up_ref[first : first + 48, :] = four[i][48:96]
        down = jnp.concatenate([piece[96:144] for piece in four], axis=0)
        down = dot_nn(swap, down).astype(bf16)
        for m in range(4):
            down_ref[48 * g : 48 * g + 48, HALF * m : HALF * m + HALF] = down[48 * m : 48 * m + 48]


def unpack(gathered):
    return pl.pallas_call(
        unpack_kernel,
        grid=(4,),
        in_specs=[
            pl.BlockSpec((192, 192), lambda s: (0, 0)),
            pl.BlockSpec((N_DP, 1, 144, HALF), lambda s: (0, s, 0, 0)),
        ],
        out_specs=[
            pl.BlockSpec((3, HALF, HALF), lambda s: (0, s // 2, s % 2)),
            pl.BlockSpec((HALF, HALF), lambda s: (s % 2, s // 2)),
            pl.BlockSpec((FF // 2, HALF), lambda s: (s // 2, s % 2)),
            pl.BlockSpec((HALF, FF // 2), lambda s: (s % 2, s // 2)),
        ],
        out_shape=[
            jax.ShapeDtypeStruct((3, D, D), bf16),
            jax.ShapeDtypeStruct((D, D), bf16),
            jax.ShapeDtypeStruct((FF, D), bf16),
            jax.ShapeDtypeStruct((D, FF), bf16),
        ],
        compiler_params=pltpu.CompilerParams(vmem_limit_bytes=48 * 1024 * 1024),
        name="unpack_weights",
    )(swap_matrix(), gathered)


def moments(values):
    mean = jnp.sum(values, axis=1, keepdims=True) * (1.0 / D)
    centered = values - mean
    spread = jnp.sum(centered * centered, axis=1, keepdims=True) * (1.0 / D)
    inverse = lax.rsqrt(spread + norm_eps)
    return centered * inverse, inverse


def norm_back(grad_norm, unit, inverse, gain):
    scaled = grad_norm * gain
    total = jnp.sum(scaled, axis=1, keepdims=True) * (1.0 / D)
    crossed = jnp.sum(scaled * unit, axis=1, keepdims=True) * (1.0 / D)
    return inverse * (scaled - total - unit * crossed)


def gelu_pair(x):
    c = 0.7978845608028654
    square = x * x
    t = jnp.tanh(c * (x + 0.044715 * (square * x)))
    half = 0.5 * (1.0 + t)
    value = x * half
    slope = half + (0.5 * x) * (1.0 - t * t) * (c + (3.0 * 0.044715 * c) * square)
    return value, slope


def layer_kernel(
    place_ref,
    lengths_ref,
    x_ref,
    n1_ref,
    gl_ref,
    og_ref,
    vec_ref,
    bqkv_ref,
    bup_ref,
    wqkv_ref,
    wout_ref,
    wup_ref,
    wdown_ref,
    result_ref,
    gin_ref,
    gqkv_out,
    gout_out,
    gup_out,
    gdown_out,
    small_out,
    bias_s,
    q_s,
    k_s,
    v_s,
    vt_s,
    kt_s,
    p_s,
    at_s,
    a_s,
    mid_s,
    n2_s,
    act_s,
    gn2_s,
    gm_s,
    ga_s,
    gq_s,
    gk_s,
    gv_s,
    gqt_s,
):
    row = place_ref[0]
    col = place_ref[1]
    row_tok = pl.ds(pl.multiple_of(row * 256, 256), 256)
    row_half = pl.ds(pl.multiple_of(row * HALF, 128), HALF)
    col_half = pl.ds(pl.multiple_of(col * HALF, 128), HALF)

    e0 = lengths_ref[0, 0]
    e1 = e0 + lengths_ref[0, 1]
    e2 = e1 + lengths_ref[0, 2]
    key_place = lax.broadcasted_iota(jnp.int32, (TOK, 1), 0)
    query_place = lax.broadcasted_iota(jnp.int32, (1, TOK), 1)

    def segment(places):
        return (
            (places >= e0).astype(jnp.int32)
            + (places >= e1).astype(jnp.int32)
            + (places >= e2).astype(jnp.int32)
        )

    allowed = (segment(key_place) == segment(query_place)) & (key_place <= query_place)
    bias_s[...] = jnp.where(allowed, 0.0, neg_large)

    n1 = n1_ref[...]
    queries = (dot_nt(n1, wqkv_ref[0]) + bqkv_ref[0:1, :]).astype(bf16)
    q_s[...] = queries * jnp.asarray(HD**-0.5, bf16)
    keys = dot_nt(n1, wqkv_ref[1]).astype(bf16)
    k_s[...] = keys
    kt_s[...] = keys.T
    values = (dot_nt(n1, wqkv_ref[2]) + bqkv_ref[2:3, :]).astype(bf16)
    v_s[...] = values
    vt_s[...] = values.T

    lane = lax.broadcasted_iota(jnp.int32, (1, 128), 1)

    def forward_pair(pair, carry):
        lanes = pl.ds(pl.multiple_of(pair * 128, 128), 128)
        q_pair = q_s[:, lanes]
        k_pair = k_s[:, lanes]
        for hh in range(2):
            mine = (lane < HD) if hh == 0 else (lane >= HD)
            q_one = jnp.where(mine, q_pair, jnp.zeros_like(q_pair))
            rows = pl.ds(pl.multiple_of(pair * 128 + hh * HD, HD), HD)
            for j in range(2):
                kn = 256 * (j + 1)
                qs = slice(256 * j, 256 * j + 256)
                scores = dot_nt(k_pair[:kn], q_one[qs]) + bias_s[:kn, qs]
                top = jnp.max(scores, axis=0, keepdims=True)
                weights = jnp.exp(scores - top)
                total = jnp.sum(weights, axis=0, keepdims=True)
                probs = (weights * (1.0 / total)).astype(bf16)
                p_s[2 * pair + hh, :kn, qs] = probs
                at_s[rows, qs] = dot_nn(vt_s[rows, :kn], probs)
        return carry

    lax.fori_loop(0, 6, forward_pair, 0)
    a_s[...] = at_s[...].T.astype(bf16)

    mid = x_ref[...].astype(f32) + dot_nt(a_s[...], wout_ref[...]) + vec_ref[4:5, :]
    mid_s[...] = mid
    unit2, inverse2 = moments(mid)
    n2_s[...] = (unit2 * vec_ref[2:3, :] + vec_ref[3:4, :]).astype(bf16)

    result_ref[...] = mid_s[row_tok, col_half] + vec_ref[5:6, col_half]
    for chunk in range(4):
        units = slice(D * chunk, D * chunk + D)
        hidden = dot_nt(n2_s[...], wup_ref[units, :]) + bup_ref[:, units]
        value, slope = gelu_pair(hidden)
        act_s[...] = value.astype(bf16)
        result_ref[...] += dot_nt(act_s[row_tok, :], wdown_ref[col_half, units])
        grad_act = dot_nn(gl_ref[...], wdown_ref[:, units])
        grad_hidden = (grad_act * slope).astype(bf16)
        part = dot_nn(grad_hidden, wup_ref[units, :])
        if chunk == 0:
            gn2_s[...] = part
        else:
            gn2_s[...] += part

        @pl.when(row == chunk // 2)
        def _():
            place = slice(D * (chunk % 2), D * (chunk % 2) + D)
            gup_out[place, :] = dot_tn(grad_hidden, n2_s[:, col_half]).astype(bf16)
            gdown_out[:, place] = dot_tn(gl_ref[:, col_half], act_s[...]).astype(bf16)
            sums = jnp.sum(grad_hidden.astype(f32), axis=0, keepdims=True).astype(bf16).astype(f32)
            for half in range(2):
                small_out[8 + 2 * (chunk % 2) + half : 9 + 2 * (chunk % 2) + half, :] = sums[
                    :, HALF * half : HALF * half + HALF
                ]

    gn2 = gn2_s[...]
    unit2, inverse2 = moments(mid_s[...])
    delta = norm_back(gn2, unit2, inverse2, vec_ref[2:3, :])
    grad_mid = delta + gl_ref[...].astype(f32)
    gm_s[...] = grad_mid.astype(bf16)
    mid_s[...] = delta


    sums_rows = jnp.concatenate(
        [
            jnp.sum(gn2 * unit2, axis=0, keepdims=True),
            jnp.sum(gn2, axis=0, keepdims=True),
            jnp.sum(grad_mid, axis=0, keepdims=True),
            jnp.sum(gl_ref[...].astype(f32), axis=0, keepdims=True),
        ],
        axis=0,
    )
    gn2_s[0:4, :] = sums_rows
    small_out[2:6, :] = gn2_s[0:4, col_half]
    ga_s[...] = dot_nn(gm_s[...], wout_ref[...]).astype(bf16)
    gout_out[...] = dot_tn(gm_s[:, col_half], a_s[:, row_half]).astype(bf16)

    def backward_pair(pair, carry):
        lanes = pl.ds(pl.multiple_of(pair * 128, 128), 128)
        q_pair = q_s[:, lanes]
        v_pair = v_s[:, lanes]
        g_pair = ga_s[:, lanes]
        grad_keys = []
        grad_values = []
        for hh in range(2):
            mine = (lane < HD) if hh == 0 else (lane >= HD)
            g_one = jnp.where(mine, g_pair, jnp.zeros_like(g_pair))
            rows = pl.ds(pl.multiple_of(pair * 128 + hh * HD, HD), HD)
            gk_parts = []
            gv_parts = []
            for j in range(2):
                kn = 256 * (j + 1)
                qs = slice(256 * j, 256 * j + 256)
                probs_low = p_s[2 * pair + hh, :kn, qs]
                probs = probs_low.astype(f32)
                product = probs * dot_nt(v_pair[:kn], g_one[qs])
                inner = jnp.sum(product, axis=0, keepdims=True)
                grad_scores = (product - probs * inner).astype(bf16)
                gv_parts.append(dot_nn(probs_low, g_pair[qs]))
                gk_parts.append(dot_nn(grad_scores, q_pair[qs]))
                gqt_s[rows, qs] = dot_nn(kt_s[rows, :kn], grad_scores)
            grad_keys.append((gk_parts[0] + gk_parts[1][:256], gk_parts[1][256:]))
            grad_values.append((gv_parts[0] + gv_parts[1][:256], gv_parts[1][256:]))
        for piece in range(2):
            ts = slice(256 * piece, 256 * piece + 256)
            gk_s[ts, lanes] = jnp.where(
                lane < HD, grad_keys[0][piece], grad_keys[1][piece]
            ).astype(bf16)
            gv_s[ts, lanes] = jnp.where(
                lane < HD, grad_values[0][piece], grad_values[1][piece]
            ).astype(bf16)
        return carry

    lax.fori_loop(0, 6, backward_pair, 0)
    gq_s[...] = (gqt_s[...].T * HD**-0.5).astype(bf16)

    n1_half = n1_ref[:, col_half]
    for j, source in enumerate((gq_s, gk_s, gv_s)):
        gqkv_out[j] = dot_tn(source[:, row_half], n1_half).astype(bf16)
    small_out[6:7, :] = jnp.sum(gq_s[:, row_half].astype(f32), axis=0, keepdims=True)
    small_out[7:8, :] = jnp.sum(gv_s[:, row_half].astype(f32), axis=0, keepdims=True)
    gn1 = (
        dot_nn(gq_s[...], wqkv_ref[0])
        + dot_nn(gk_s[...], wqkv_ref[1])
        + dot_nn(gv_s[...], wqkv_ref[2])
    )
    unit1, inverse1 = moments(x_ref[...].astype(f32))
    mid_s[...] += norm_back(gn1, unit1, inverse1, vec_ref[0:1, :])
    gn2_s[0:2, :] = jnp.concatenate(
        [jnp.sum(gn1 * unit1, axis=0, keepdims=True), jnp.sum(gn1, axis=0, keepdims=True)], axis=0
    )
    small_out[0:2, :] = gn2_s[0:2, col_half]
    small_out[12:16, :] = jnp.zeros((4, HALF), f32)
    gin_ref[...] = mid_s[row_tok, col_half] + og_ref[...]


def layer(place, lengths, *operands):
    smem = pl.BlockSpec(memory_space=pltpu.SMEM)
    whole = pl.BlockSpec(memory_space=VMEM)
    return pl.pallas_call(
        layer_kernel,
        in_specs=[smem, smem] + [whole] * len(operands),
        out_specs=[whole] * 7,
        out_shape=[
            jax.ShapeDtypeStruct((256, HALF), f32),
            jax.ShapeDtypeStruct((256, HALF), f32),
            jax.ShapeDtypeStruct((3, HALF, HALF), bf16),
            jax.ShapeDtypeStruct((HALF, HALF), bf16),
            jax.ShapeDtypeStruct((FF // 2, HALF), bf16),
            jax.ShapeDtypeStruct((HALF, FF // 2), bf16),
            jax.ShapeDtypeStruct((16, HALF), f32),
        ],
        scratch_shapes=[
            VMEM((TOK, TOK), f32),
            VMEM((TOK, D), bf16),
            VMEM((TOK, D), bf16),
            VMEM((TOK, D), bf16),
            VMEM((D, TOK), bf16),
            VMEM((D, TOK), bf16),
            VMEM((12, TOK, TOK), bf16),
            VMEM((D, TOK), f32),
            VMEM((TOK, D), bf16),
            VMEM((TOK, D), f32),
            VMEM((TOK, D), bf16),
            VMEM((TOK, D), bf16),
            VMEM((TOK, D), f32),
            VMEM((TOK, D), bf16),
            VMEM((TOK, D), bf16),
            VMEM((TOK, D), bf16),
            VMEM((TOK, D), bf16),
            VMEM((TOK, D), bf16),
            VMEM((D, TOK), f32),
        ],
        compiler_params=pltpu.CompilerParams(vmem_limit_bytes=60 * 1024 * 1024),
        name="layer",
    )(place, lengths, *operands)


def pack_kernel(core_ref, swap_ref, qkv_ref, out_ref, up_ref, down_ref, small_ref, buf_ref):
    core = core_ref[0]
    swap = swap_ref[...]
    small = small_ref[...].astype(bf16)
    for g in range(8):
        rows = slice(48 * g, 48 * g + 48)
        attn = jnp.concatenate([qkv_ref[j, rows, :] for j in range(3)] + [out_ref[rows, :]], axis=0)
        attn = dot_nn(swap, attn).astype(bf16)
        down = jnp.concatenate(
            [down_ref[rows, HALF * m : HALF * m + HALF] for m in range(4)], axis=0
        )
        down = dot_nn(swap, down).astype(bf16)
        for i in range(4):
            to = 4 * g + i
            slot = jnp.bitwise_xor(core, to % 2)
            part = slice(48 * i, 48 * i + 48)
            buf_ref[slot, to // 2, 0:48, :] = attn[part]
            buf_ref[slot, to // 2, 48:96, :] = up_ref[48 * to : 48 * to + 48, :]
            buf_ref[slot, to // 2, 96:144, :] = down[part]
            buf_ref[slot, to // 2, 144:160, :] = small


def pack(core, *grads):
    whole = pl.BlockSpec(memory_space=VMEM)
    return pl.pallas_call(
        pack_kernel,
        in_specs=[pl.BlockSpec(memory_space=pltpu.SMEM)] + [whole] * 6,
        out_specs=whole,
        out_shape=jax.ShapeDtypeStruct((2, 16, 160, HALF), bf16),
        compiler_params=pltpu.CompilerParams(vmem_limit_bytes=48 * 1024 * 1024),
        name="pack_gradients",
    )(core, swap_matrix(), *grads)


def adam_update(master, first_old, second_old, gradient, step_rate):
    first_new = beta_one * first_old + (1.0 - beta_one) * gradient
    second_new = beta_two * second_old + (1.0 - beta_two) * gradient * gradient
    ratio = (
        first_new
        / (1.0 - beta_one**STEP)
        / (jnp.sqrt(second_new / (1.0 - beta_two**STEP)) + adam_eps)
    )
    return (second_new, master - step_rate * (ratio + decay_rate * master))


def on_device(
    block_in,
    out_grad,
    seq_lengths,
    weight_qkv,
    first_qkv,
    second_qkv,
    weight_out,
    first_out,
    second_out,
    weight_up,
    first_up,
    second_up,
    weight_down,
    first_down,
    second_down,
    col_params,
    first_col,
    second_col,
    bias_qv,
    first_qv,
    second_qv,
    bias_up,
    first_bup,
    second_bup,
):
    shard = jnp.concatenate(
        [
            weight_qkv.transpose(1, 3, 2, 0).reshape(36, HALF),
            weight_out.transpose(2, 1, 0).reshape(12, HALF),
            weight_up.transpose(2, 1, 0).reshape(48, HALF),
            weight_down.transpose(2, 1, 0).reshape(12, 4, HALF).transpose(1, 0, 2).reshape(48, HALF),
        ],
        axis=0,
    ).astype(bf16)
    gathered = lax.all_gather(shard, ALL, axis=0, tiled=False).reshape(N_DP, 4, 144, HALF)

    small = jnp.concatenate(
        [col_params.reshape(72), bias_qv.reshape(24), bias_up.reshape(48)]
    ).astype(bf16)
    smalls = lax.all_gather(small, ALL, axis=0, tiled=False).reshape(N_DP, 2, 2, 144).astype(f32)
    vec = smalls[:, 0, :, 0:72].reshape(N_DP, 2, 6, 12).transpose(2, 1, 0, 3).reshape(6, D)
    vec = jnp.concatenate([vec, jnp.zeros((2, D), f32)], axis=0)
    bqv = smalls[:, :, 0, 72:96].reshape(N_DP, 2, 2, 12).transpose(2, 1, 0, 3).reshape(2, D)
    bqkv = jnp.stack([bqv[0], jnp.zeros_like(bqv[0]), bqv[1]])
    bup = smalls[:, :, 0, 96:144].transpose(1, 0, 2).reshape(1, FF)

    def whole_rows(block):
        four = lax.all_gather(block, ("row", "col"), axis=0, tiled=False)
        return four.reshape(2, 2, 256, HALF).transpose(0, 2, 1, 3).reshape(TOK, D)

    rows_full = whole_rows(block_in)
    grad_full = whole_rows(out_grad.astype(bf16))
    unit_one, _ = moments(rows_full.astype(f32))
    normed_one = (unit_one * vec[0:1] + vec[1:2]).astype(bf16)

    place = jnp.stack([lax.axis_index("row"), lax.axis_index("col")]).astype(jnp.int32)
    wqkv, wout, wup, wdown = unpack(gathered)
    result, grad_in, gqkv, gout, gup, gdown, gsmall = layer(
        place,
        seq_lengths,
        rows_full,
        normed_one,
        grad_full,
        out_grad,
        vec,
        bqkv,
        bup,
        wqkv,
        wout,
        wup,
        wdown,
    )

    core = lax.axis_index("core").astype(jnp.int32)
    packed = pack(core.reshape(1), gqkv, gout, gup, gdown, gsmall)
    other = lax.ppermute(packed[1], "core", [(0, 1), (1, 0)])
    both = (packed[0].astype(f32) + other.astype(f32)).astype(bf16)
    parts = lax.all_to_all(both, ("y", "x"), 0, 0, tiled=True)
    total = jnp.sum(parts.astype(f32), axis=0)

    data = lax.axis_index(DP)
    own = lax.dynamic_slice_in_dim(total[144:152], data * 12, 12, 1)
    total_bup = lax.dynamic_slice_in_dim(total[152:156].reshape(1, FF // 2), data * 48, 48, 1)
    gradients = (
        total[0:36].reshape(3, 12, 1, HALF).transpose(3, 0, 2, 1),
        total[36:48].reshape(12, 1, HALF).transpose(2, 1, 0),
        total[48:96].reshape(48, 1, HALF).transpose(2, 1, 0),
        total[96:144].reshape(4, 12, HALF).transpose(1, 0, 2).reshape(12, 1, 1536).transpose(2, 1, 0),
        own[0:6].reshape(6, 1, 12),
        own[6:8].reshape(2, 1, 12),
        total_bup,
    )
    masters = (weight_qkv, weight_out, weight_up, weight_down, col_params, bias_qv, bias_up)
    firsts = (first_qkv, first_out, first_up, first_down, first_col, first_qv, first_bup)
    seconds = (second_qkv, second_out, second_up, second_down, second_col, second_qv, second_bup)
    outputs = [result, grad_in]
    for master, first_old, second_old, gradient, step_rate in zip(
        masters, firsts, seconds, gradients, step_rates
    ):
        second_new, updated = adam_update(master, first_old, second_old, gradient, step_rate)
        outputs += [gradient, second_new, updated]
    return tuple(outputs)


def solution(mesh):
    fine = Mesh(mesh.devices.reshape(4, 4, 2, 2, 2), ALL)
    qkv_spec = P("col", None, "row", DP)
    out_spec = P("row", "col", DP)
    up_spec = P("col", "row", DP)
    down_spec = P("row", "col", DP)
    col_spec = P(None, "col", DP)
    qv_spec = P(None, "row", DP)
    bup_spec = P("row", DP)
    rows_spec = P(DP + ("row",), "col")
    params = (qkv_spec, out_spec, up_spec, down_spec, col_spec, qv_spec, bup_spec)
    triples = tuple(spec for spec in params for _ in range(3))
    return jax.shard_map(
        on_device,
        mesh=fine,
        in_specs=(rows_spec, rows_spec, P(DP, None)) + triples,
        out_specs=(rows_spec, rows_spec) + triples,
        check_vma=False,
    )
```

```python
import functools

import jax
import jax.numpy as jnp
import numpy as np
from jax import lax
from jax.experimental import pallas as pl
from jax.experimental.pallas import tpu as pltpu
from jax.sharding import Mesh
from jax.sharding import PartitionSpec as P

HD = 64
D = 768
HALF = 384
FF = 3072
TOK = 512
N_DP = 32
STEP = 10

norm_eps = 1e-05
beta_one = 0.9
beta_two = 0.999
adam_eps = 1e-08
decay_rate = 0.1
neg_large = -1e30
step_rates = (0.25, 0.4, 0.25, 0.25, 0.3, 0.3, 0.3)

DP = ("y", "x", "core")
ALL = ("y", "x", "core", "row", "col")
bf16 = jnp.bfloat16
f32 = jnp.float32
VMEM = pltpu.VMEM


def swap_matrix():
    places = np.arange(192).reshape(4, 4, 12).transpose(1, 0, 2).reshape(192)
    return jnp.asarray(np.eye(192, dtype=np.float32)[places], dtype=bf16)


def dot_nn(a, b):
    return lax.dot_general(a, b, (((1,), (0,)), ((), ())), preferred_element_type=f32)


def dot_nt(a, b):
    return lax.dot_general(a, b, (((1,), (1,)), ((), ())), preferred_element_type=f32)


def dot_tn(a, b):
    return lax.dot_general(a, b, (((0,), (0,)), ((), ())), preferred_element_type=f32)


def masters_kernel(qkv_ref, out_ref, up_ref, down_ref, shard_ref):
    shard_ref[0:48, :] = jnp.concatenate([qkv_ref[:, 0, :], out_ref[:, 0, :]], axis=0).astype(bf16)
    shard_ref[48:96, :] = up_ref[...].astype(bf16)
    shard_ref[96:144, :] = jnp.concatenate(
        [down_ref[:, 0, HALF * m : HALF * m + HALF] for m in range(4)], axis=0
    ).astype(bf16)


def pack_masters(qkv, out, up, down):
    whole = pl.BlockSpec(memory_space=VMEM)
    return pl.pallas_call(
        masters_kernel,
        in_specs=[whole] * 4,
        out_specs=whole,
        out_shape=jax.ShapeDtypeStruct((144, HALF), bf16),
        name="pack_masters",
    )(qkv, out, up, down)


def moments(values):
    mean = jnp.sum(values, axis=1, keepdims=True) * (1.0 / D)
    centered = values - mean
    spread = jnp.sum(centered * centered, axis=1, keepdims=True) * (1.0 / D)
    inverse = lax.rsqrt(spread + norm_eps)
    return centered * inverse, inverse


def norm_back(grad_norm, unit, inverse, gain):
    scaled = grad_norm * gain
    total = jnp.sum(scaled, axis=1, keepdims=True) * (1.0 / D)
    crossed = jnp.sum(scaled * unit, axis=1, keepdims=True) * (1.0 / D)
    return inverse * (scaled - total - unit * crossed)


def gelu_pair(x):
    c = 0.7978845608028654
    square = x * x
    t = jnp.tanh(c * (x + 0.044715 * (square * x)))
    half = 0.5 * (1.0 + t)
    value = x * half
    slope = half + (0.5 * x) * (1.0 - t * t) * (c + (3.0 * 0.044715 * c) * square)
    return value, slope


def layer_kernel(
    place_ref,
    lengths_ref,
    x_ref,
    n1_ref,
    gl_ref,
    og_ref,
    vec_ref,
    bqkv_ref,
    bup_ref,
    swap_ref,
    gathered_ref,
    result_ref,
    gin_ref,
    keep_out,
    send_out,
    load_sem,
    store_sem,
    stage_s,
    wqkv_s,
    wout_s,
    wup_s,
    wdown_s,
    gattn_s,
    gup_s,
    gdown_s,
    small_s,
    buf_s,
    bias_s,
    q_s,
    k_s,
    v_s,
    vt_s,
    kt_s,
    p_s,
    at_s,
    a_s,
    mid_s,
    n2_s,
    act_s,
    gn2_s,
    gm_s,
    ga_s,
    gq_s,
    gk_s,
    gv_s,
    gqt_s,
):
    row = place_ref[0]
    col = place_ref[1]
    row_tok = pl.ds(pl.multiple_of(row * 256, 256), 256)
    row_half = pl.ds(pl.multiple_of(row * HALF, 128), HALF)
    col_half = pl.ds(pl.multiple_of(col * HALF, 128), HALF)

    core = place_ref[2]
    swap = swap_ref[...]
    load_attn = [
        pltpu.make_async_copy(gathered_ref.at[:, s, 0:48, :], stage_s.at[s], load_sem.at[s])
        for s in range(4)
    ]
    load_up = [
        pltpu.make_async_copy(
            gathered_ref.at[:, s, 48:96, :],
            wup_s.at[32 * (s // 2) : 32 * (s // 2) + 32, :, HALF * (s % 2) : HALF * (s % 2) + HALF],
            load_sem.at[4 + s],
        )
        for s in range(4)
    ]
    load_down = [
        pltpu.make_async_copy(gathered_ref.at[:, s, 96:144, :], stage_s.at[s], load_sem.at[8 + s])
        for s in range(4)
    ]
    for copy in load_attn + load_up:
        copy.start()

    def unswapped(s, g):
        block = stage_s[s, 4 * g : 4 * g + 4].reshape(192, HALF)
        return dot_nn(swap, block).astype(bf16)

    e0 = lengths_ref[0, 0]
    e1 = e0 + lengths_ref[0, 1]
    e2 = e1 + lengths_ref[0, 2]
    key_place = lax.broadcasted_iota(jnp.int32, (TOK, 1), 0)
    query_place = lax.broadcasted_iota(jnp.int32, (1, TOK), 1)

    def segment(places):
        return (
            (places >= e0).astype(jnp.int32)
            + (places >= e1).astype(jnp.int32)
            + (places >= e2).astype(jnp.int32)
        )

    allowed = (segment(key_place) == segment(query_place)) & (key_place <= query_place)
    bias_s[...] = jnp.where(allowed, 0.0, neg_large)

    for s in range(4):
        load_attn[s].wait()
        outer = HALF * (s // 2)
        inner = HALF * (s % 2)
        for g in range(8):
            block = unswapped(s, g)
            for j in range(3):
                wqkv_s[j, outer + 48 * g : outer + 48 * g + 48, inner : inner + HALF] = block[
                    48 * j : 48 * j + 48
                ]
            wout_s[inner + 48 * g : inner + 48 * g + 48, outer : outer + HALF] = block[144:192]
        load_down[s].start()

    n1 = n1_ref[...]
    queries = (dot_nt(n1, wqkv_s[0]) + bqkv_ref[0:1, :]).astype(bf16)
    q_s[...] = queries * jnp.asarray(HD**-0.5, bf16)
    keys = dot_nt(n1, wqkv_s[1]).astype(bf16)
    k_s[...] = keys
    kt_s[...] = keys.T
    values = (dot_nt(n1, wqkv_s[2]) + bqkv_ref[2:3, :]).astype(bf16)
    v_s[...] = values
    vt_s[...] = values.T

    lane = lax.broadcasted_iota(jnp.int32, (1, 128), 1)

    def forward_pair(pair, carry):
        lanes = pl.ds(pl.multiple_of(pair * 128, 128), 128)
        q_pair = q_s[:, lanes]
        k_pair = k_s[:, lanes]
        for hh in range(2):
            mine = (lane < HD) if hh == 0 else (lane >= HD)
            q_one = jnp.where(mine, q_pair, jnp.zeros_like(q_pair))
            rows = pl.ds(pl.multiple_of(pair * 128 + hh * HD, HD), HD)
            for j in range(2):
                kn = 256 * (j + 1)
                qs = slice(256 * j, 256 * j + 256)
                scores = dot_nt(k_pair[:kn], q_one[qs]) + bias_s[:kn, qs]
                top = jnp.max(scores, axis=0, keepdims=True)
                weights = jnp.exp(scores - top)
                total = jnp.sum(weights, axis=0, keepdims=True)
                probs = (weights * (1.0 / total)).astype(bf16)
                p_s[2 * pair + hh, :kn, qs] = probs
                at_s[rows, qs] = dot_nn(vt_s[rows, :kn], probs)
        return carry

    lax.fori_loop(0, 6, forward_pair, 0)
    a_s[...] = at_s[...].T.astype(bf16)

    mid = x_ref[...].astype(f32) + dot_nt(a_s[...], wout_s[...]) + vec_ref[4:5, :]
    mid_s[...] = mid
    unit2, inverse2 = moments(mid)
    n2_s[...] = (unit2 * vec_ref[2:3, :] + vec_ref[3:4, :]).astype(bf16)

    for s in range(4):
        load_up[s].wait()
        load_down[s].wait()
        outer = HALF * (s % 2)
        inner = (FF // 2) * (s // 2)
        for g in range(8):
            block = unswapped(s, g)
            for m in range(4):
                wdown_s[
                    outer + 48 * g : outer + 48 * g + 48, inner + HALF * m : inner + HALF * m + HALF
                ] = block[48 * m : 48 * m + 48]
    result_ref[...] = mid_s[row_tok, col_half] + vec_ref[5:6, col_half]
    for chunk in range(4):
        units = slice(D * chunk, D * chunk + D)
        up = wup_s[16 * chunk : 16 * chunk + 16].reshape(D, D)
        hidden = dot_nt(n2_s[...], up) + bup_ref[:, units]
        value, slope = gelu_pair(hidden)
        act_s[...] = value.astype(bf16)
        result_ref[...] += dot_nt(act_s[row_tok, :], wdown_s[col_half, units])
        grad_act = dot_nn(gl_ref[...], wdown_s[:, units])
        grad_hidden = (grad_act * slope).astype(bf16)
        part = dot_nn(grad_hidden, up)
        if chunk == 0:
            gn2_s[...] = part
        else:
            gn2_s[...] += part

        @pl.when(row == chunk // 2)
        def _():
            place = slice(D * (chunk % 2), D * (chunk % 2) + D)
            gup_s[place, :] = dot_tn(grad_hidden, n2_s[:, col_half]).astype(bf16)
            gdown_s[:, place] = dot_tn(gl_ref[:, col_half], act_s[...]).astype(bf16)
            sums = jnp.sum(grad_hidden.astype(f32), axis=0, keepdims=True).astype(bf16).astype(f32)
            for half in range(2):
                small_s[8 + 2 * (chunk % 2) + half : 9 + 2 * (chunk % 2) + half, :] = sums[
                    :, HALF * half : HALF * half + HALF
                ]

    gn2 = gn2_s[...]
    unit2, inverse2 = moments(mid_s[...])
    delta = norm_back(gn2, unit2, inverse2, vec_ref[2:3, :])
    grad_mid = delta + gl_ref[...].astype(f32)
    gm_s[...] = grad_mid.astype(bf16)
    mid_s[...] = delta


    sums_rows = jnp.concatenate(
        [
            jnp.sum(gn2 * unit2, axis=0, keepdims=True),
            jnp.sum(gn2, axis=0, keepdims=True),
            jnp.sum(grad_mid, axis=0, keepdims=True),
            jnp.sum(gl_ref[...].astype(f32), axis=0, keepdims=True),
        ],
        axis=0,
    )
    gn2_s[0:4, :] = sums_rows
    small_s[2:6, :] = gn2_s[0:4, col_half]
    ga_s[...] = dot_nn(gm_s[...], wout_s[...]).astype(bf16)
    gattn_s[3] = dot_tn(gm_s[:, col_half], a_s[:, row_half]).astype(bf16)

    def backward_pair(pair, carry):
        lanes = pl.ds(pl.multiple_of(pair * 128, 128), 128)
        q_pair = q_s[:, lanes]
        v_pair = v_s[:, lanes]
        g_pair = ga_s[:, lanes]
        grad_keys = []
        grad_values = []
        for hh in range(2):
            mine = (lane < HD) if hh == 0 else (lane >= HD)
            g_one = jnp.where(mine, g_pair, jnp.zeros_like(g_pair))
            rows = pl.ds(pl.multiple_of(pair * 128 + hh * HD, HD), HD)
            gk_parts = []
            gv_parts = []
            for j in range(2):
                kn = 256 * (j + 1)
                qs = slice(256 * j, 256 * j + 256)
                probs_low = p_s[2 * pair + hh, :kn, qs]
                probs = probs_low.astype(f32)
                product = probs * dot_nt(v_pair[:kn], g_one[qs])
                inner = jnp.sum(product, axis=0, keepdims=True)
                grad_scores = (product - probs * inner).astype(bf16)
                gv_parts.append(dot_nn(probs_low, g_pair[qs]))
                gk_parts.append(dot_nn(grad_scores, q_pair[qs]))
                gqt_s[rows, qs] = dot_nn(kt_s[rows, :kn], grad_scores)
            grad_keys.append((gk_parts[0] + gk_parts[1][:256], gk_parts[1][256:]))
            grad_values.append((gv_parts[0] + gv_parts[1][:256], gv_parts[1][256:]))
        for piece in range(2):
            ts = slice(256 * piece, 256 * piece + 256)
            gk_s[ts, lanes] = jnp.where(
                lane < HD, grad_keys[0][piece], grad_keys[1][piece]
            ).astype(bf16)
            gv_s[ts, lanes] = jnp.where(
                lane < HD, grad_values[0][piece], grad_values[1][piece]
            ).astype(bf16)
        return carry

    lax.fori_loop(0, 6, backward_pair, 0)
    gq_s[...] = (gqt_s[...].T * HD**-0.5).astype(bf16)

    n1_half = n1_ref[:, col_half]
    for j, source in enumerate((gq_s, gk_s, gv_s)):
        gattn_s[j] = dot_tn(source[:, row_half], n1_half).astype(bf16)
    small_s[6:7, :] = jnp.sum(gq_s[:, row_half].astype(f32), axis=0, keepdims=True)
    small_s[7:8, :] = jnp.sum(gv_s[:, row_half].astype(f32), axis=0, keepdims=True)
    gn1 = (
        dot_nn(gq_s[...], wqkv_s[0])
        + dot_nn(gk_s[...], wqkv_s[1])
        + dot_nn(gv_s[...], wqkv_s[2])
    )
    unit1, inverse1 = moments(x_ref[...].astype(f32))
    mid_s[...] += norm_back(gn1, unit1, inverse1, vec_ref[0:1, :])
    gn2_s[0:2, :] = jnp.concatenate(
        [jnp.sum(gn1 * unit1, axis=0, keepdims=True), jnp.sum(gn1, axis=0, keepdims=True)], axis=0
    )
    small_s[0:2, :] = gn2_s[0:2, col_half]
    small_s[12:16, :] = jnp.zeros((4, HALF), f32)
    gin_ref[...] = mid_s[row_tok, col_half] + og_ref[...]

    small = small_s[...].astype(bf16)
    for g in range(8):
        rows = slice(48 * g, 48 * g + 48)
        attn = dot_nn(swap, gattn_s[:, rows, :].reshape(192, HALF)).astype(bf16)
        down = jnp.concatenate([gdown_s[rows, HALF * m : HALF * m + HALF] for m in range(4)], axis=0)
        down = dot_nn(swap, down).astype(bf16)
        for i in range(4):
            to = 4 * g + i
            slot = jnp.bitwise_xor(core, to % 2)
            part = slice(48 * i, 48 * i + 48)
            buf_s[slot, to // 2, 0:48, :] = attn[part]
            buf_s[slot, to // 2, 48:96, :] = gup_s[48 * to : 48 * to + 48, :]
            buf_s[slot, to // 2, 96:144, :] = down[part]
            buf_s[slot, to // 2, 144:160, :] = small
    store_send = pltpu.make_async_copy(buf_s.at[1], send_out, store_sem.at[0])
    store_keep = pltpu.make_async_copy(buf_s.at[0], keep_out, store_sem.at[1])
    store_send.start()
    store_keep.start()
    store_send.wait()
    store_keep.wait()


def layer(place, lengths, *operands):
    smem = pl.BlockSpec(memory_space=pltpu.SMEM)
    whole = pl.BlockSpec(memory_space=VMEM)
    anywhere = pl.BlockSpec(memory_space=pl.ANY)
    return pl.pallas_call(
        layer_kernel,
        in_specs=[smem, smem] + [whole] * (len(operands) - 1) + [anywhere],
        out_specs=[whole, whole, anywhere, anywhere],
        out_shape=[
            jax.ShapeDtypeStruct((256, HALF), f32),
            jax.ShapeDtypeStruct((256, HALF), f32),
            jax.ShapeDtypeStruct((16, 160, HALF), bf16),
            jax.ShapeDtypeStruct((16, 160, HALF), bf16),
        ],
        scratch_shapes=[
            pltpu.SemaphoreType.DMA((12,)),
            pltpu.SemaphoreType.DMA((2,)),
            VMEM((4, N_DP, 48, HALF), bf16),
            VMEM((3, D, D), bf16),
            VMEM((D, D), bf16),
            VMEM((64, 48, D), bf16),
            VMEM((D, FF), bf16),
            VMEM((4, HALF, HALF), bf16),
            VMEM((FF // 2, HALF), bf16),
            VMEM((HALF, FF // 2), bf16),
            VMEM((16, HALF), f32),
            VMEM((2, 16, 160, HALF), bf16),
            VMEM((TOK, TOK), f32),
            VMEM((TOK, D), bf16),
            VMEM((TOK, D), bf16),
            VMEM((TOK, D), bf16),
            VMEM((D, TOK), bf16),
            VMEM((D, TOK), bf16),
            VMEM((12, TOK, TOK), bf16),
            VMEM((D, TOK), f32),
            VMEM((TOK, D), bf16),
            VMEM((TOK, D), f32),
            VMEM((TOK, D), bf16),
            VMEM((TOK, D), bf16),
            VMEM((TOK, D), f32),
            VMEM((TOK, D), bf16),
            VMEM((TOK, D), bf16),
            VMEM((TOK, D), bf16),
            VMEM((TOK, D), bf16),
            VMEM((TOK, D), bf16),
            VMEM((D, TOK), f32),
        ],
        compiler_params=pltpu.CompilerParams(vmem_limit_bytes=60 * 1024 * 1024),
        name="layer",
    )(place, lengths, *operands)


def adam_kernel(data_ref, *refs):
    parts_ref = refs[0]
    masters, firsts, seconds = refs[1:8], refs[8:15], refs[15:22]
    grads, news, updates = refs[22:29], refs[29:36], refs[36:43]
    total = parts_ref[0].astype(f32)
    for i in range(1, 16):
        total = total + parts_ref[i].astype(f32)
    data = data_ref[0]
    small = pltpu.roll(total[144:152], HALF - data * 12, 1)
    wide = jnp.concatenate([total[152 + m : 153 + m] for m in range(4)], axis=1)
    wide = pltpu.roll(jnp.broadcast_to(wide, (8, FF // 2)), FF // 2 - data * 48, 1)
    gradients = (
        total[0:36].reshape(36, 1, HALF),
        total[36:48].reshape(12, 1, HALF),
        total[48:96],
        jnp.concatenate([total[96 + 12 * m : 108 + 12 * m] for m in range(4)], axis=1).reshape(
            12, 1, 4 * HALF
        ),
        small[0:6, 0:12].reshape(6, 1, 12),
        small[6:8, 0:12].reshape(2, 1, 12),
        wide[0:1, 0:48],
    )
    for i in range(7):
        second_new, updated = adam_update(
            masters[i][...], firsts[i][...], seconds[i][...], gradients[i], step_rates[i]
        )
        grads[i][...] = gradients[i]
        news[i][...] = second_new
        updates[i][...] = updated


def update_masters(data, parts, masters, firsts, seconds):
    whole = pl.BlockSpec(memory_space=VMEM)
    shapes = [jax.ShapeDtypeStruct(m.shape, f32) for m in masters]
    results = pl.pallas_call(
        adam_kernel,
        in_specs=[pl.BlockSpec(memory_space=pltpu.SMEM)] + [whole] * 22,
        out_specs=[whole] * 21,
        out_shape=shapes * 3,
        compiler_params=pltpu.CompilerParams(vmem_limit_bytes=32 * 1024 * 1024),
        name="update_masters",
    )(data, parts, *masters, *firsts, *seconds)
    return results[0:7], results[7:14], results[14:21]


def adam_update(master, first_old, second_old, gradient, step_rate):
    first_new = beta_one * first_old + (1.0 - beta_one) * gradient
    second_new = beta_two * second_old + (1.0 - beta_two) * gradient * gradient
    ratio = (
        first_new
        / (1.0 - beta_one**STEP)
        / (jnp.sqrt(second_new / (1.0 - beta_two**STEP)) + adam_eps)
    )
    return (second_new, master - step_rate * (ratio + decay_rate * master))


def on_device(
    block_in,
    out_grad,
    seq_lengths,
    weight_qkv,
    first_qkv,
    second_qkv,
    weight_out,
    first_out,
    second_out,
    weight_up,
    first_up,
    second_up,
    weight_down,
    first_down,
    second_down,
    col_params,
    first_col,
    second_col,
    bias_qv,
    first_qv,
    second_qv,
    bias_up,
    first_bup,
    second_bup,
):
    def flat(qkv, out, up, down, col, qv, bup):
        return (
            qkv.transpose(1, 3, 2, 0).reshape(36, 1, HALF),
            out.transpose(2, 1, 0),
            up.transpose(1, 2, 0).reshape(48, HALF),
            down.transpose(2, 1, 0),
            col,
            qv,
            bup,
        )

    def unflat(qkv, out, up, down, col, qv, bup):
        return (
            qkv.reshape(3, 12, 1, HALF).transpose(3, 0, 2, 1),
            out.transpose(2, 1, 0),
            up.reshape(1, 48, HALF).transpose(2, 0, 1),
            down.transpose(2, 1, 0),
            col,
            qv,
            bup,
        )

    masters = flat(weight_qkv, weight_out, weight_up, weight_down, col_params, bias_qv, bias_up)
    firsts = flat(first_qkv, first_out, first_up, first_down, first_col, first_qv, first_bup)
    seconds = flat(second_qkv, second_out, second_up, second_down, second_col, second_qv, second_bup)
    gathered = lax.all_gather(pack_masters(*masters[:4]), ALL, axis=0, tiled=False)
    gathered = gathered.reshape(N_DP, 4, 144, HALF)

    small = jnp.concatenate(
        [col_params.reshape(72), bias_qv.reshape(24), bias_up.reshape(48), jnp.zeros(240, f32)]
    ).astype(bf16)
    small = jnp.concatenate([small.reshape(1, HALF), jnp.zeros((15, HALF), bf16)], axis=0)
    four = lax.all_gather(
        jnp.concatenate([block_in, small], axis=0), ("row", "col"), axis=0, tiled=False
    )

    def whole_rows(four):
        return four.reshape(2, 2, 256, HALF).transpose(0, 2, 1, 3).reshape(TOK, D)

    rows_full = whole_rows(four[:, 0:256])
    smalls = lax.all_gather(four[:, 256, 0:144], DP, axis=0, tiled=False)
    smalls = smalls.reshape(N_DP, 2, 2, 144).astype(f32)
    vec = smalls[:, 0, :, 0:72].reshape(N_DP, 2, 6, 12).transpose(2, 1, 0, 3).reshape(6, D)
    vec = jnp.concatenate([vec, jnp.zeros((2, D), f32)], axis=0)
    bqv = smalls[:, :, 0, 72:96].reshape(N_DP, 2, 2, 12).transpose(2, 1, 0, 3).reshape(2, D)
    bqkv = jnp.stack([bqv[0], jnp.zeros_like(bqv[0]), bqv[1]])
    bup = smalls[:, :, 0, 96:144].transpose(1, 0, 2).reshape(1, FF)
    grad_full = whole_rows(
        lax.all_gather(out_grad.astype(bf16), ("row", "col"), axis=0, tiled=False)
    )
    unit_one, _ = moments(rows_full.astype(f32))
    normed_one = (unit_one * vec[0:1] + vec[1:2]).astype(bf16)

    place = jnp.stack([lax.axis_index("row"), lax.axis_index("col"), lax.axis_index("core")])
    result, grad_in, keep, send = layer(
        place.astype(jnp.int32),
        seq_lengths,
        rows_full,
        normed_one,
        grad_full,
        out_grad,
        vec,
        bqkv,
        bup,
        swap_matrix(),
        gathered,
    )

    other = lax.ppermute(send, "core", [(0, 1), (1, 0)])
    both = (keep.astype(f32) + other.astype(f32)).astype(bf16)
    parts = lax.all_to_all(both, ("y", "x"), 0, 0, tiled=True)
    data = lax.axis_index(DP).astype(jnp.int32).reshape(1)
    grads, news, updates = update_masters(data, parts, masters, firsts, seconds)
    outputs = [result, grad_in]
    for triple in zip(unflat(*grads), unflat(*news), unflat(*updates)):
        outputs += triple
    return tuple(outputs)


def solution(mesh):
    fine = Mesh(mesh.devices.reshape(4, 4, 2, 2, 2), ALL)
    qkv_spec = P("col", None, "row", DP)
    out_spec = P("row", "col", DP)
    up_spec = P("col", "row", DP)
    down_spec = P("row", "col", DP)
    col_spec = P(None, "col", DP)
    qv_spec = P(None, "row", DP)
    bup_spec = P("row", DP)
    rows_spec = P(DP + ("row",), "col")
    params = (qkv_spec, out_spec, up_spec, down_spec, col_spec, qv_spec, bup_spec)
    triples = tuple(spec for spec in params for _ in range(3))
    return jax.shard_map(
        on_device,
        mesh=fine,
        in_specs=(rows_spec, rows_spec, P(DP, None)) + triples,
        out_specs=(rows_spec, rows_spec) + triples,
        check_vma=False,
    )
```

```python
import functools

import jax
import jax.numpy as jnp
import numpy as np
from jax import lax
from jax.experimental import pallas as pl
from jax.experimental.pallas import tpu as pltpu
from jax.sharding import Mesh
from jax.sharding import PartitionSpec as P

HD = 64
D = 768
HALF = 384
FF = 3072
TOK = 512
QW = 256
QB = 2
N_DP = 32
STEP = 10

norm_eps = 1e-05
beta_one = 0.9
beta_two = 0.999
adam_eps = 1e-08
decay_rate = 0.1
neg_large = -1e30
step_rates = (0.25, 0.4, 0.25, 0.25, 0.3, 0.3, 0.3)

DP = ("y", "x", "core")
ALL = ("y", "x", "core", "row", "col")
bf16 = jnp.bfloat16
f32 = jnp.float32
VMEM = pltpu.VMEM


def swap_matrix():
    places = np.arange(192).reshape(4, 4, 12).transpose(1, 0, 2).reshape(192)
    return jnp.asarray(np.eye(192, dtype=np.float32)[places], dtype=bf16)


def dot_nn(a, b):
    return lax.dot_general(a, b, (((1,), (0,)), ((), ())), preferred_element_type=f32)


def dot_nt(a, b):
    return lax.dot_general(a, b, (((1,), (1,)), ((), ())), preferred_element_type=f32)


def dot_tn(a, b):
    return lax.dot_general(a, b, (((0,), (0,)), ((), ())), preferred_element_type=f32)


def masters_kernel(qkv_ref, out_ref, up_ref, down_ref, shard_ref):
    shard_ref[0:48, :] = jnp.concatenate([qkv_ref[:, 0, :], out_ref[:, 0, :]], axis=0).astype(bf16)
    shard_ref[48:96, :] = up_ref[...].astype(bf16)
    shard_ref[96:144, :] = jnp.concatenate(
        [down_ref[:, 0, HALF * m : HALF * m + HALF] for m in range(4)], axis=0
    ).astype(bf16)


def pack_masters(qkv, out, up, down):
    whole = pl.BlockSpec(memory_space=VMEM)
    return pl.pallas_call(
        masters_kernel,
        in_specs=[whole] * 4,
        out_specs=whole,
        out_shape=jax.ShapeDtypeStruct((144, HALF), bf16),
        name="pack_masters",
    )(qkv, out, up, down)


def moments(values):
    mean = jnp.sum(values, axis=1, keepdims=True) * (1.0 / D)
    centered = values - mean
    spread = jnp.sum(centered * centered, axis=1, keepdims=True) * (1.0 / D)
    inverse = lax.rsqrt(spread + norm_eps)
    return centered * inverse, inverse


def norm_back(grad_norm, unit, inverse, gain):
    scaled = grad_norm * gain
    total = jnp.sum(scaled, axis=1, keepdims=True) * (1.0 / D)
    crossed = jnp.sum(scaled * unit, axis=1, keepdims=True) * (1.0 / D)
    return inverse * (scaled - total - unit * crossed)


def gelu_pair(x):
    c = 0.7978845608028654
    square = x * x
    t = jnp.tanh(c * (x + 0.044715 * (square * x)))
    half = 0.5 * (1.0 + t)
    value = x * half
    slope = half + (0.5 * x) * (1.0 - t * t) * (c + (3.0 * 0.044715 * c) * square)
    return value, slope


def layer_kernel(
    place_ref,
    lengths_ref,
    x_ref,
    n1_ref,
    gl_ref,
    og_ref,
    vec_ref,
    bqkv_ref,
    bup_ref,
    swap_ref,
    gathered_ref,
    result_ref,
    gin_ref,
    keep_out,
    send_out,
    load_sem,
    store_sem,
    stage_s,
    wqkv_s,
    wout_s,
    wup_s,
    wdown_s,
    gattn_s,
    gup_s,
    gdown_s,
    small_s,
    buf_s,
    bias_s,
    q_s,
    k_s,
    v_s,
    vt_s,
    kt_s,
    p_s,
    at_s,
    a_s,
    mid_s,
    n2_s,
    act_s,
    gh_s,
    gn2_s,
    gqt_s,
):
    row = place_ref[0]
    col = place_ref[1]
    row_tok = pl.ds(pl.multiple_of(row * 256, 256), 256)
    row_half = pl.ds(pl.multiple_of(row * HALF, 128), HALF)
    col_half = pl.ds(pl.multiple_of(col * HALF, 128), HALF)

    core = place_ref[2]
    swap = swap_ref[...]
    load_attn = [
        pltpu.make_async_copy(gathered_ref.at[:, s, 0:48, :], stage_s.at[s], load_sem.at[s])
        for s in range(4)
    ]
    load_up = [
        pltpu.make_async_copy(
            gathered_ref.at[:, s, 48:96, :],
            wup_s.at[32 * (s // 2) : 32 * (s // 2) + 32, :, HALF * (s % 2) : HALF * (s % 2) + HALF],
            load_sem.at[4 + s],
        )
        for s in range(4)
    ]
    load_down = [
        pltpu.make_async_copy(gathered_ref.at[:, s, 96:144, :], stage_s.at[s], load_sem.at[8 + s])
        for s in range(4)
    ]
    for copy in load_attn + load_up:
        copy.start()

    def unswapped(s, g):
        block = stage_s[s, 4 * g : 4 * g + 4].reshape(192, HALF)
        return dot_nn(swap, block).astype(bf16)

    e0 = lengths_ref[0, 0]
    e1 = e0 + lengths_ref[0, 1]
    e2 = e1 + lengths_ref[0, 2]
    key_place = lax.broadcasted_iota(jnp.int32, (TOK, 1), 0)
    query_place = lax.broadcasted_iota(jnp.int32, (1, TOK), 1)

    def segment(places):
        return (
            (places >= e0).astype(jnp.int32)
            + (places >= e1).astype(jnp.int32)
            + (places >= e2).astype(jnp.int32)
        )

    allowed = (segment(key_place) == segment(query_place)) & (key_place <= query_place)
    bias_s[...] = jnp.where(allowed, 0.0, neg_large)

    for s in range(4):
        load_attn[s].wait()
        outer = HALF * (s // 2)
        inner = HALF * (s % 2)
        for g in range(8):
            block = unswapped(s, g)
            for j in range(3):
                wqkv_s[j, outer + 48 * g : outer + 48 * g + 48, inner : inner + HALF] = block[
                    48 * j : 48 * j + 48
                ]
            wout_s[inner + 48 * g : inner + 48 * g + 48, outer : outer + HALF] = block[144:192]
        load_down[s].start()

    n1 = n1_ref[...]
    queries = (dot_nt(n1, wqkv_s[0]) + bqkv_ref[0:1, :]).astype(bf16)
    q_s[...] = queries * jnp.asarray(HD**-0.5, bf16)
    keys = dot_nt(n1, wqkv_s[1]).astype(bf16)
    k_s[...] = keys
    kt_s[...] = keys.T
    values = (dot_nt(n1, wqkv_s[2]) + bqkv_ref[2:3, :]).astype(bf16)
    v_s[...] = values
    vt_s[...] = values.T

    lane = lax.broadcasted_iota(jnp.int32, (1, 128), 1)

    for pair in range(6):
        lanes = slice(pair * 128, pair * 128 + 128)
        q_pair = q_s[:, lanes]
        k_pair = k_s[:, lanes]
        for hh in range(2):
            mine = (lane < HD) if hh == 0 else (lane >= HD)
            q_one = jnp.where(mine, q_pair, jnp.zeros_like(q_pair))
            rows = slice(pair * 128 + hh * HD, pair * 128 + hh * HD + HD)
            for j in range(QB):
                kn = QW * (j + 1)
                qs = slice(QW * j, QW * j + QW)
                scores = dot_nt(k_pair[:kn], q_one[qs]) + bias_s[:kn, qs]
                top = jnp.max(scores, axis=0, keepdims=True)
                weights = jnp.exp(scores - top)
                total = jnp.sum(weights, axis=0, keepdims=True)
                probs = (weights * (1.0 / total)).astype(bf16)
                p_s[2 * pair + hh, :kn, qs] = probs
                at_s[rows, qs] = dot_nn(vt_s[rows, :kn], probs)

    a_s[...] = at_s[...].T.astype(bf16)

    mid = x_ref[...].astype(f32) + dot_nt(a_s[...], wout_s[...]) + vec_ref[4:5, :]
    mid_s[...] = mid
    unit2, inverse2 = moments(mid)
    n2_s[...] = (unit2 * vec_ref[2:3, :] + vec_ref[3:4, :]).astype(bf16)

    for s in range(4):
        load_up[s].wait()
        load_down[s].wait()
        outer = HALF * (s % 2)
        inner = (FF // 2) * (s // 2)
        for g in range(8):
            block = unswapped(s, g)
            for m in range(4):
                wdown_s[
                    outer + 48 * g : outer + 48 * g + 48, inner + HALF * m : inner + HALF * m + HALF
                ] = block[48 * m : 48 * m + 48]
    for chunk in range(4):
        units = slice(D * chunk, D * chunk + D)
        up = wup_s[16 * chunk : 16 * chunk + 16].reshape(D, D)
        for tile in range(2):
            ts = slice(256 * tile, 256 * tile + 256)
            hidden = dot_nt(n2_s[ts, :], up) + bup_ref[:, units]
            value, slope = gelu_pair(hidden)
            act_s[ts, units] = value.astype(bf16)
            grad_act = dot_nn(gl_ref[ts, :], wdown_s[:, units])
            grad_hidden = (grad_act * slope).astype(bf16)
            gh_s[ts, units] = grad_hidden
    for tile in range(2):
        ts = slice(256 * tile, 256 * tile + 256)
        gn2_s[ts, :] = dot_nn(gh_s[ts, :], wup_s[...].reshape(FF, D))
    result_ref[...] = (
        mid_s[row_tok, col_half]
        + vec_ref[5:6, col_half]
        + dot_nt(act_s[row_tok, :], wdown_s[col_half, :])
    )
    row_units = pl.ds(pl.multiple_of(row * (FF // 2), 128), FF // 2)
    gup_s[...] = dot_tn(gh_s[:, row_units], n2_s[:, col_half]).astype(bf16)
    gdown_s[...] = dot_tn(gl_ref[:, col_half], act_s[:, row_units]).astype(bf16)
    sums = jnp.sum(gh_s[:, row_units].astype(f32), axis=0, keepdims=True)
    for part in range(4):
        small_s[8 + part : 9 + part, :] = sums[:, HALF * part : HALF * part + HALF]

    ga_s = gh_s.at[:, 0:D]
    gq_s = gh_s.at[:, D : 2 * D]
    gk_s = gh_s.at[:, 2 * D : 3 * D]
    gv_s = gh_s.at[:, 3 * D : 4 * D]
    gm_s = act_s.at[:, 0:D]
    gn2 = gn2_s[...]
    unit2, inverse2 = moments(mid_s[...])
    delta = norm_back(gn2, unit2, inverse2, vec_ref[2:3, :])
    grad_mid = delta + gl_ref[...].astype(f32)
    gm_s[...] = grad_mid.astype(bf16)
    mid_s[...] = delta


    sums_rows = jnp.concatenate(
        [
            jnp.sum(gn2 * unit2, axis=0, keepdims=True),
            jnp.sum(gn2, axis=0, keepdims=True),
            jnp.sum(grad_mid, axis=0, keepdims=True),
            jnp.sum(gl_ref[...].astype(f32), axis=0, keepdims=True),
        ],
        axis=0,
    )
    gn2_s[0:4, :] = sums_rows
    small_s[2:6, :] = gn2_s[0:4, col_half]
    ga_s[...] = dot_nn(gm_s[...], wout_s[...]).astype(bf16)
    gattn_s[3] = dot_tn(gm_s[:, col_half], a_s[:, row_half]).astype(bf16)

    for pair in range(6):
        lanes = slice(pair * 128, pair * 128 + 128)
        q_pair = q_s[:, lanes]
        v_pair = v_s[:, lanes]
        g_pair = ga_s[:, lanes]
        grad_keys = []
        grad_values = []
        for hh in range(2):
            mine = (lane < HD) if hh == 0 else (lane >= HD)
            g_one = jnp.where(mine, g_pair, jnp.zeros_like(g_pair))
            rows = slice(pair * 128 + hh * HD, pair * 128 + hh * HD + HD)
            gk_parts = []
            gv_parts = []
            for j in range(2):
                kn = 256 * (j + 1)
                qs = slice(256 * j, 256 * j + 256)
                probs_low = p_s[2 * pair + hh, :kn, qs]
                probs = probs_low.astype(f32)
                product = probs * dot_nt(v_pair[:kn], g_one[qs])
                inner = jnp.sum(product, axis=0, keepdims=True)
                grad_scores = (product - probs * inner).astype(bf16)
                gv_parts.append(dot_nn(probs_low, g_pair[qs]))
                gk_parts.append(dot_nn(grad_scores, q_pair[qs]))
                gqt_s[rows, qs] = dot_nn(kt_s[rows, :kn], grad_scores)
            grad_keys.append((gk_parts[0] + gk_parts[1][:256], gk_parts[1][256:]))
            grad_values.append((gv_parts[0] + gv_parts[1][:256], gv_parts[1][256:]))
        for piece in range(2):
            ts = slice(256 * piece, 256 * piece + 256)
            gk_s[ts, lanes] = jnp.where(
                lane < HD, grad_keys[0][piece], grad_keys[1][piece]
            ).astype(bf16)
            gv_s[ts, lanes] = jnp.where(
                lane < HD, grad_values[0][piece], grad_values[1][piece]
            ).astype(bf16)

    gq_s[...] = (gqt_s[...].T * HD**-0.5).astype(bf16)

    n1_half = n1_ref[:, col_half]
    for j, source in enumerate((gq_s, gk_s, gv_s)):
        gattn_s[j] = dot_tn(source[:, row_half], n1_half).astype(bf16)
    small_s[6:7, :] = jnp.sum(gq_s[:, row_half].astype(f32), axis=0, keepdims=True)
    small_s[7:8, :] = jnp.sum(gv_s[:, row_half].astype(f32), axis=0, keepdims=True)
    gn1 = (
        dot_nn(gq_s[...], wqkv_s[0])
        + dot_nn(gk_s[...], wqkv_s[1])
        + dot_nn(gv_s[...], wqkv_s[2])
    )
    unit1, inverse1 = moments(x_ref[...].astype(f32))
    mid_s[...] += norm_back(gn1, unit1, inverse1, vec_ref[0:1, :])
    gn2_s[0:2, :] = jnp.concatenate(
        [jnp.sum(gn1 * unit1, axis=0, keepdims=True), jnp.sum(gn1, axis=0, keepdims=True)], axis=0
    )
    small_s[0:2, :] = gn2_s[0:2, col_half]
    small_s[12:16, :] = jnp.zeros((4, HALF), f32)
    gin_ref[...] = mid_s[row_tok, col_half] + og_ref[...]

    small = small_s[...].astype(bf16)
    for g in range(8):
        rows = slice(48 * g, 48 * g + 48)
        attn = dot_nn(swap, gattn_s[:, rows, :].reshape(192, HALF)).astype(bf16)
        down = jnp.concatenate([gdown_s[rows, HALF * m : HALF * m + HALF] for m in range(4)], axis=0)
        down = dot_nn(swap, down).astype(bf16)
        for i in range(4):
            to = 4 * g + i
            slot = jnp.bitwise_xor(core, to % 2)
            part = slice(48 * i, 48 * i + 48)
            buf_s[slot, to // 2, 0:48, :] = attn[part]
            buf_s[slot, to // 2, 48:96, :] = gup_s[48 * to : 48 * to + 48, :]
            buf_s[slot, to // 2, 96:144, :] = down[part]
            buf_s[slot, to // 2, 144:160, :] = small
    store_send = pltpu.make_async_copy(buf_s.at[1], send_out, store_sem.at[0])
    store_keep = pltpu.make_async_copy(buf_s.at[0], keep_out, store_sem.at[1])
    store_send.start()
    store_keep.start()
    store_send.wait()
    store_keep.wait()


def layer(place, lengths, *operands):
    smem = pl.BlockSpec(memory_space=pltpu.SMEM)
    whole = pl.BlockSpec(memory_space=VMEM)
    anywhere = pl.BlockSpec(memory_space=pl.ANY)
    return pl.pallas_call(
        layer_kernel,
        in_specs=[smem, smem] + [whole] * (len(operands) - 1) + [anywhere],
        out_specs=[whole, whole, anywhere, anywhere],
        out_shape=[
            jax.ShapeDtypeStruct((256, HALF), f32),
            jax.ShapeDtypeStruct((256, HALF), f32),
            jax.ShapeDtypeStruct((16, 160, HALF), bf16),
            jax.ShapeDtypeStruct((16, 160, HALF), bf16),
        ],
        scratch_shapes=[
            pltpu.SemaphoreType.DMA((12,)),
            pltpu.SemaphoreType.DMA((2,)),
            VMEM((4, N_DP, 48, HALF), bf16),
            VMEM((3, D, D), bf16),
            VMEM((D, D), bf16),
            VMEM((64, 48, D), bf16),
            VMEM((D, FF), bf16),
            VMEM((4, HALF, HALF), bf16),
            VMEM((FF // 2, HALF), bf16),
            VMEM((HALF, FF // 2), bf16),
            VMEM((16, HALF), f32),
            VMEM((2, 16, 160, HALF), bf16),
            VMEM((TOK, TOK), f32),
            VMEM((TOK, D), bf16),
            VMEM((TOK, D), bf16),
            VMEM((TOK, D), bf16),
            VMEM((D, TOK), bf16),
            VMEM((D, TOK), bf16),
            VMEM((12, TOK, TOK), bf16),
            VMEM((D, TOK), f32),
            VMEM((TOK, D), bf16),
            VMEM((TOK, D), f32),
            VMEM((TOK, D), bf16),
            VMEM((TOK, FF), bf16),
            VMEM((TOK, FF), bf16),
            VMEM((TOK, D), f32),
            VMEM((D, TOK), f32),
        ],
        compiler_params=pltpu.CompilerParams(vmem_limit_bytes=60 * 1024 * 1024),
        name="layer",
    )(place, lengths, *operands)


def adam_kernel(data_ref, *refs):
    parts_ref = refs[0]
    masters, firsts, seconds = refs[1:8], refs[8:15], refs[15:22]
    grads, news, updates = refs[22:29], refs[29:36], refs[36:43]
    total = parts_ref[0].astype(f32)
    for i in range(1, 16):
        total = total + parts_ref[i].astype(f32)
    data = data_ref[0]
    small = pltpu.roll(total[144:152], HALF - data * 12, 1)
    wide = jnp.concatenate([total[152 + m : 153 + m] for m in range(4)], axis=1)
    wide = pltpu.roll(jnp.broadcast_to(wide, (8, FF // 2)), FF // 2 - data * 48, 1)
    gradients = (
        total[0:36].reshape(36, 1, HALF),
        total[36:48].reshape(12, 1, HALF),
        total[48:96],
        jnp.concatenate([total[96 + 12 * m : 108 + 12 * m] for m in range(4)], axis=1).reshape(
            12, 1, 4 * HALF
        ),
        small[0:6, 0:12].reshape(6, 1, 12),
        small[6:8, 0:12].reshape(2, 1, 12),
        wide[0:1, 0:48],
    )
    for i in range(7):
        second_new, updated = adam_update(
            masters[i][...], firsts[i][...], seconds[i][...], gradients[i], step_rates[i]
        )
        grads[i][...] = gradients[i]
        news[i][...] = second_new
        updates[i][...] = updated


def update_masters(data, parts, masters, firsts, seconds):
    whole = pl.BlockSpec(memory_space=VMEM)
    shapes = [jax.ShapeDtypeStruct(m.shape, f32) for m in masters]
    results = pl.pallas_call(
        adam_kernel,
        in_specs=[pl.BlockSpec(memory_space=pltpu.SMEM)] + [whole] * 22,
        out_specs=[whole] * 21,
        out_shape=shapes * 3,
        compiler_params=pltpu.CompilerParams(vmem_limit_bytes=32 * 1024 * 1024),
        name="update_masters",
    )(data, parts, *masters, *firsts, *seconds)
    return results[0:7], results[7:14], results[14:21]


def adam_update(master, first_old, second_old, gradient, step_rate):
    first_new = beta_one * first_old + (1.0 - beta_one) * gradient
    second_new = beta_two * second_old + (1.0 - beta_two) * gradient * gradient
    ratio = (
        first_new
        / (1.0 - beta_one**STEP)
        / (jnp.sqrt(second_new / (1.0 - beta_two**STEP)) + adam_eps)
    )
    return (second_new, master - step_rate * (ratio + decay_rate * master))


def on_device(
    block_in,
    out_grad,
    seq_lengths,
    weight_qkv,
    first_qkv,
    second_qkv,
    weight_out,
    first_out,
    second_out,
    weight_up,
    first_up,
    second_up,
    weight_down,
    first_down,
    second_down,
    col_params,
    first_col,
    second_col,
    bias_qv,
    first_qv,
    second_qv,
    bias_up,
    first_bup,
    second_bup,
):
    def flat(qkv, out, up, down, col, qv, bup):
        return (
            qkv.transpose(1, 3, 2, 0).reshape(36, 1, HALF),
            out.transpose(2, 1, 0),
            up.transpose(1, 2, 0).reshape(48, HALF),
            down.transpose(2, 1, 0),
            col,
            qv,
            bup,
        )

    def unflat(qkv, out, up, down, col, qv, bup):
        return (
            qkv.reshape(3, 12, 1, HALF).transpose(3, 0, 2, 1),
            out.transpose(2, 1, 0),
            up.reshape(1, 48, HALF).transpose(2, 0, 1),
            down.transpose(2, 1, 0),
            col,
            qv,
            bup,
        )

    masters = flat(weight_qkv, weight_out, weight_up, weight_down, col_params, bias_qv, bias_up)
    firsts = flat(first_qkv, first_out, first_up, first_down, first_col, first_qv, first_bup)
    seconds = flat(second_qkv, second_out, second_up, second_down, second_col, second_qv, second_bup)
    gathered = lax.all_gather(pack_masters(*masters[:4]), ALL, axis=0, tiled=False)
    gathered = gathered.reshape(N_DP, 4, 144, HALF)

    small = jnp.concatenate(
        [col_params.reshape(72), bias_qv.reshape(24), bias_up.reshape(48), jnp.zeros(240, f32)]
    ).astype(bf16)
    small = jnp.concatenate([small.reshape(1, HALF), jnp.zeros((15, HALF), bf16)], axis=0)
    four = lax.all_gather(
        jnp.concatenate([block_in, small], axis=0), ("row", "col"), axis=0, tiled=False
    )

    def whole_rows(four):
        return four.reshape(2, 2, 256, HALF).transpose(0, 2, 1, 3).reshape(TOK, D)

    rows_full = whole_rows(four[:, 0:256])
    smalls = lax.all_gather(four[:, 256, 0:144], DP, axis=0, tiled=False)
    smalls = smalls.reshape(N_DP, 2, 2, 144).astype(f32)
    vec = smalls[:, 0, :, 0:72].reshape(N_DP, 2, 6, 12).transpose(2, 1, 0, 3).reshape(6, D)
    vec = jnp.concatenate([vec, jnp.zeros((2, D), f32)], axis=0)
    bqv = smalls[:, :, 0, 72:96].reshape(N_DP, 2, 2, 12).transpose(2, 1, 0, 3).reshape(2, D)
    bqkv = jnp.stack([bqv[0], jnp.zeros_like(bqv[0]), bqv[1]])
    bup = smalls[:, :, 0, 96:144].transpose(1, 0, 2).reshape(1, FF)
    grad_full = whole_rows(
        lax.all_gather(out_grad.astype(bf16), ("row", "col"), axis=0, tiled=False)
    )
    unit_one, _ = moments(rows_full.astype(f32))
    normed_one = (unit_one * vec[0:1] + vec[1:2]).astype(bf16)

    place = jnp.stack([lax.axis_index("row"), lax.axis_index("col"), lax.axis_index("core")])
    result, grad_in, keep, send = layer(
        place.astype(jnp.int32),
        seq_lengths,
        rows_full,
        normed_one,
        grad_full,
        out_grad,
        vec,
        bqkv,
        bup,
        swap_matrix(),
        gathered,
    )

    other = lax.ppermute(send, "core", [(0, 1), (1, 0)])
    both = (keep.astype(f32) + other.astype(f32)).astype(bf16)
    parts = lax.all_to_all(both, ("y", "x"), 0, 0, tiled=True)
    data = lax.axis_index(DP).astype(jnp.int32).reshape(1)
    grads, news, updates = update_masters(data, parts, masters, firsts, seconds)
    outputs = [result, grad_in]
    for triple in zip(unflat(*grads), unflat(*news), unflat(*updates)):
        outputs += triple
    return tuple(outputs)


def solution(mesh):
    fine = Mesh(mesh.devices.reshape(4, 4, 2, 2, 2), ALL)
    qkv_spec = P("col", None, "row", DP)
    out_spec = P("row", "col", DP)
    up_spec = P("col", "row", DP)
    down_spec = P("row", "col", DP)
    col_spec = P(None, "col", DP)
    qv_spec = P(None, "row", DP)
    bup_spec = P("row", DP)
    rows_spec = P(DP + ("row",), "col")
    params = (qkv_spec, out_spec, up_spec, down_spec, col_spec, qv_spec, bup_spec)
    triples = tuple(spec for spec in params for _ in range(3))
    return jax.shard_map(
        on_device,
        mesh=fine,
        in_specs=(rows_spec, rows_spec, P(DP, None)) + triples,
        out_specs=(rows_spec, rows_spec) + triples,
        check_vma=False,
    )
```

```python
import functools

import jax
import jax.numpy as jnp
import numpy as np
from jax import lax
from jax.experimental import pallas as pl
from jax.experimental.pallas import tpu as pltpu
from jax.sharding import Mesh
from jax.sharding import PartitionSpec as P

HD = 64
D = 768
HALF = 384
FF = 3072
TOK = 512
QW = 256
QB = 2
N_DP = 32
STEP = 10

norm_eps = 1e-05
beta_one = 0.9
beta_two = 0.999
adam_eps = 1e-08
decay_rate = 0.1
neg_large = -1e30
step_rates = (0.25, 0.4, 0.25, 0.25, 0.3, 0.3, 0.3)

DP = ("y", "x", "core")
ALL = ("y", "x", "core", "row", "col")
bf16 = jnp.bfloat16
f32 = jnp.float32
VMEM = pltpu.VMEM


def swap_matrix():
    places = np.arange(192).reshape(4, 4, 12).transpose(1, 0, 2).reshape(192)
    return jnp.asarray(np.eye(192, dtype=np.float32)[places], dtype=bf16)


def dot_nn(a, b):
    return lax.dot_general(a, b, (((1,), (0,)), ((), ())), preferred_element_type=f32)


def dot_nt(a, b):
    return lax.dot_general(a, b, (((1,), (1,)), ((), ())), preferred_element_type=f32)


def dot_tn(a, b):
    return lax.dot_general(a, b, (((0,), (0,)), ((), ())), preferred_element_type=f32)


def masters_kernel(qkv_ref, out_ref, up_ref, down_ref, shard_ref):
    shard_ref[0:48, :] = jnp.concatenate([qkv_ref[:, 0, :], out_ref[:, 0, :]], axis=0).astype(bf16)
    shard_ref[48:96, :] = up_ref[...].astype(bf16)
    shard_ref[96:144, :] = jnp.concatenate(
        [down_ref[:, 0, HALF * m : HALF * m + HALF] for m in range(4)], axis=0
    ).astype(bf16)


def pack_masters(qkv, out, up, down):
    whole = pl.BlockSpec(memory_space=VMEM)
    return pl.pallas_call(
        masters_kernel,
        in_specs=[whole] * 4,
        out_specs=whole,
        out_shape=jax.ShapeDtypeStruct((144, HALF), bf16),
        name="pack_masters",
    )(qkv, out, up, down)


def moments(values):
    mean = jnp.sum(values, axis=1, keepdims=True) * (1.0 / D)
    centered = values - mean
    spread = jnp.sum(centered * centered, axis=1, keepdims=True) * (1.0 / D)
    inverse = lax.rsqrt(spread + norm_eps)
    return centered * inverse, inverse


def norm_back(grad_norm, unit, inverse, gain):
    scaled = grad_norm * gain
    total = jnp.sum(scaled, axis=1, keepdims=True) * (1.0 / D)
    crossed = jnp.sum(scaled * unit, axis=1, keepdims=True) * (1.0 / D)
    return inverse * (scaled - total - unit * crossed)


def gelu_pair(x):
    c = 0.7978845608028654
    square = x * x
    t = jnp.tanh(x * (c + (0.044715 * c) * square))
    half = 0.5 + 0.5 * t
    value = x * half
    slope = half + value * (1.0 - t) * (c + (3.0 * 0.044715 * c) * square)
    return value, slope


def layer_kernel(
    place_ref,
    lengths_ref,
    x_hbm,
    n1_ref,
    gl_hbm,
    og_hbm,
    vec_ref,
    bqkv_ref,
    bup_ref,
    swap_ref,
    gathered_ref,
    result_ref,
    part_ref,
    small_s,
    keep_out,
    send_out,
    gqkv_out,
    wqkv_out,
    load_sem,
    store_sem,
    x_ref,
    gl_ref,
    og_ref,
    stage_s,
    wqkv_s,
    wout_s,
    wup_s,
    wdown_s,
    buf_s,
    bias_s,
    q_s,
    k_s,
    v_s,
    vt_s,
    kt_s,
    p_s,
    at_s,
    share_s,
    a_s,
    mid_s,
    n2_s,
    act_s,
    gh_s,
    gn2_s,
    gqt_s,
):
    row = place_ref[0]
    col = place_ref[1]
    row_tok = pl.ds(pl.multiple_of(row * 256, 256), 256)
    row_half = pl.ds(pl.multiple_of(row * HALF, 128), HALF)
    col_half = pl.ds(pl.multiple_of(col * HALF, 128), HALF)

    core = place_ref[2]
    swap = swap_ref[...]
    load_attn = [
        pltpu.make_async_copy(gathered_ref.at[:, s, 0:48, :], stage_s.at[s], load_sem.at[s])
        for s in range(4)
    ]
    load_up = [
        pltpu.make_async_copy(
            gathered_ref.at[:, s, 48:96, :],
            wup_s.at[32 * (s // 2) : 32 * (s // 2) + 32, :, HALF * (s % 2) : HALF * (s % 2) + HALF],
            load_sem.at[4 + s],
        )
        for s in range(4)
    ]
    load_down = [
        pltpu.make_async_copy(gathered_ref.at[:, s, 96:144, :], stage_s.at[s], load_sem.at[8 + s])
        for s in range(4)
    ]
    load_rows = [
        pltpu.make_async_copy(source, target, load_sem.at[12 + i])
        for i, (source, target) in enumerate(((x_hbm, x_ref), (gl_hbm, gl_ref), (og_hbm, og_ref)))
    ]
    for copy in load_attn + load_rows:
        copy.start()

    def unswapped(s, g):
        block = stage_s[s, 4 * g : 4 * g + 4].reshape(192, HALF)
        return dot_nn(swap, block).astype(bf16)

    e0 = lengths_ref[0, 0]
    e1 = e0 + lengths_ref[0, 1]
    e2 = e1 + lengths_ref[0, 2]
    key_place = lax.broadcasted_iota(jnp.int32, (TOK, 1), 0)
    query_place = lax.broadcasted_iota(jnp.int32, (1, TOK), 1)

    def segment(places):
        return (
            (places >= e0).astype(jnp.int32)
            + (places >= e1).astype(jnp.int32)
            + (places >= e2).astype(jnp.int32)
        )

    allowed = (segment(key_place) == segment(query_place)) & (key_place <= query_place)
    bias_s[...] = jnp.where(allowed, 0.0, neg_large)

    for s in range(4):
        load_attn[s].wait()
        outer = HALF * (s // 2)
        inner = HALF * (s % 2)
        for g in range(8):
            block = unswapped(s, g)
            for j in range(3):
                wqkv_s[j, outer + 48 * g : outer + 48 * g + 48, inner : inner + HALF] = block[
                    48 * j : 48 * j + 48
                ]
            wout_s[inner + 48 * g : inner + 48 * g + 48, outer : outer + HALF] = block[144:192]
        load_up[s].start()
        load_down[s].start()

    n1 = n1_ref[...]
    queries = (dot_nt(n1, wqkv_s[0]) + bqkv_ref[0:1, :]).astype(bf16)
    q_s[...] = queries * jnp.asarray(HD**-0.5, bf16)
    keys = dot_nt(n1, wqkv_s[1]).astype(bf16)
    k_s[...] = keys
    kt_s[...] = keys.T
    values = (dot_nt(n1, wqkv_s[2]) + bqkv_ref[2:3, :]).astype(bf16)
    store_wqkv = pltpu.make_async_copy(wqkv_s, wqkv_out, store_sem.at[2])
    store_wqkv.start()
    v_s[...] = values
    vt_s[...] = values.T

    lane = lax.broadcasted_iota(jnp.int32, (1, 128), 1)

    for pair in range(6):
        lanes = slice(pair * 128, pair * 128 + 128)
        q_pair = q_s[:, lanes]
        k_pair = k_s[:, lanes]
        for hh in range(2):
            mine = (lane < HD) if hh == 0 else (lane >= HD)
            q_one = jnp.where(mine, q_pair, jnp.zeros_like(q_pair))
            rows = slice(pair * 128 + hh * HD, pair * 128 + hh * HD + HD)
            for j in range(QB):
                kn = QW * (j + 1)
                qs = slice(QW * j, QW * j + QW)
                scores = dot_nt(k_pair[:kn], q_one[qs]) + bias_s[:kn, qs]
                top = jnp.max(scores, axis=0, keepdims=True)
                weights = jnp.exp(scores - top)
                share = 1.0 / jnp.sum(weights, axis=0, keepdims=True)
                weights = weights.astype(bf16)
                p_s[2 * pair + hh, :kn, qs] = weights
                share_s[2 * pair + hh : 2 * pair + hh + 1, qs] = share
                at_s[rows, qs] = (dot_nn(vt_s[rows, :kn], weights) * share).astype(bf16)

    a_s[...] = at_s[...].T
    share_t = share_s[...].T

    for copy in load_rows:
        copy.wait()
    mid = x_ref[...].astype(f32) + dot_nt(a_s[...], wout_s[...]) + vec_ref[4:5, :]
    mid_s[...] = mid
    unit2, inverse2 = moments(mid)
    n2_s[...] = (unit2 * vec_ref[2:3, :] + vec_ref[3:4, :]).astype(bf16)

    for s in range(4):
        load_up[s].wait()
        load_down[s].wait()
        outer = HALF * (s % 2)
        inner = (FF // 2) * (s // 2)
        for g in range(8):
            block = unswapped(s, g)
            for m in range(4):
                wdown_s[
                    outer + 48 * g : outer + 48 * g + 48, inner + HALF * m : inner + HALF * m + HALF
                ] = block[48 * m : 48 * m + 48]
    for chunk in range(4):
        units = slice(D * chunk, D * chunk + D)
        up = wup_s[16 * chunk : 16 * chunk + 16].reshape(D, D)
        for tile in range(2):
            ts = slice(256 * tile, 256 * tile + 256)
            hidden = dot_nt(n2_s[ts, :], up) + bup_ref[:, units]
            value, slope = gelu_pair(hidden)
            act_s[ts, units] = value.astype(bf16)
            grad_act = dot_nn(gl_ref[ts, :], wdown_s[:, units])
            grad_hidden = (grad_act * slope).astype(bf16)
            gh_s[ts, units] = grad_hidden
    for tile in range(2):
        ts = slice(256 * tile, 256 * tile + 256)
        gn2_s[ts, :] = dot_nn(gh_s[ts, :], wup_s[...].reshape(FF, D))
    result_ref[...] = (
        mid_s[row_tok, col_half]
        + vec_ref[5:6, col_half]
        + dot_nt(act_s[row_tok, :], wdown_s[col_half, :])
    )
    row_units = pl.ds(pl.multiple_of(row * (FF // 2), 128), FF // 2)
    grad_up = dot_tn(gh_s[:, row_units], n2_s[:, col_half]).astype(bf16)
    stage_s[0] = grad_up.reshape(N_DP, 48, HALF)
    for m in range(4):
        quarter = pl.ds(pl.multiple_of(row * (FF // 2) + HALF * m, 128), HALF)
        grad_down = dot_tn(gl_ref[:, col_half], act_s[:, quarter]).astype(bf16)
        stage_s[1, 8 * m : 8 * m + 8] = grad_down.reshape(8, 48, HALF)
    sums = jnp.sum(gh_s[:, row_units].astype(f32), axis=0, keepdims=True)
    for part in range(4):
        small_s[8 + part : 9 + part, :] = sums[:, HALF * part : HALF * part + HALF]

    ga_s = gh_s.at[:, 0:D]
    gq_s = gh_s.at[:, D : 2 * D]
    gk_s = gh_s.at[:, 2 * D : 3 * D]
    gv_s = gh_s.at[:, 3 * D : 4 * D]
    gm_s = act_s.at[:, 0:D]
    gn2 = gn2_s[...]
    unit2, inverse2 = moments(mid_s[...])
    delta = norm_back(gn2, unit2, inverse2, vec_ref[2:3, :])
    grad_mid = delta + gl_ref[...].astype(f32)
    gm_s[...] = grad_mid.astype(bf16)
    mid_s[...] = delta


    sums_rows = jnp.concatenate(
        [
            jnp.sum(gn2 * unit2, axis=0, keepdims=True),
            jnp.sum(gn2, axis=0, keepdims=True),
            jnp.sum(grad_mid, axis=0, keepdims=True),
            jnp.sum(gl_ref[...].astype(f32), axis=0, keepdims=True),
        ],
        axis=0,
    )
    gn2_s[0:4, :] = sums_rows
    small_s[2:6, :] = gn2_s[0:4, col_half]
    ga_s[...] = dot_nn(gm_s[...], wout_s[...]).astype(bf16)

    def put_attn(j, grad):
        stage_s[2, 8 * j : 8 * j + 8] = grad.astype(bf16).reshape(8, 48, HALF)

    put_attn(3, dot_tn(gm_s[:, col_half], a_s[:, row_half]))

    for pair in range(6):
        lanes = slice(pair * 128, pair * 128 + 128)
        q_pair = q_s[:, lanes]
        v_pair = v_s[:, lanes]
        g_pair = ga_s[:, lanes]
        grad_keys = []
        grad_values = []
        for hh in range(2):
            mine = (lane < HD) if hh == 0 else (lane >= HD)
            head = 2 * pair + hh
            g_all = (g_pair.astype(f32) * share_t[:, head : head + 1]).astype(bf16)
            g_one = jnp.where(mine, g_all, jnp.zeros_like(g_all))
            rows = slice(pair * 128 + hh * HD, pair * 128 + hh * HD + HD)
            gk_parts = []
            gv_parts = []
            for j in range(2):
                kn = 256 * (j + 1)
                qs = slice(256 * j, 256 * j + 256)
                weights_low = p_s[head, :kn, qs]
                weights = weights_low.astype(f32)
                grad_probs = dot_nt(v_pair[:kn], g_one[qs])
                inner = jnp.sum(weights * grad_probs, axis=0, keepdims=True)
                inner = inner * share_s[head : head + 1, qs]
                grad_scores = (weights * (grad_probs - inner)).astype(bf16)
                gv_parts.append(dot_nn(weights_low, g_all[qs]))
                gk_parts.append(dot_nn(grad_scores, q_pair[qs]))
                gqt_s[rows, qs] = (dot_nn(kt_s[rows, :kn], grad_scores) * HD**-0.5).astype(bf16)
            grad_keys.append((gk_parts[0] + gk_parts[1][:256], gk_parts[1][256:]))
            grad_values.append((gv_parts[0] + gv_parts[1][:256], gv_parts[1][256:]))
        for piece in range(2):
            ts = slice(256 * piece, 256 * piece + 256)
            gk_s[ts, lanes] = jnp.where(
                lane < HD, grad_keys[0][piece], grad_keys[1][piece]
            ).astype(bf16)
            gv_s[ts, lanes] = jnp.where(
                lane < HD, grad_values[0][piece], grad_values[1][piece]
            ).astype(bf16)

    gq_s[...] = gqt_s[...].T
    store_gqkv = pltpu.make_async_copy(gh_s.at[:, D : 4 * D], gqkv_out, store_sem.at[3])
    store_gqkv.start()

    n1_half = n1_ref[:, col_half]
    row_rows = pl.ds(pl.multiple_of(row * HALF, HALF), HALF)
    put_attn(0, dot_nn(gqt_s[row_rows, :], n1_half))
    put_attn(1, dot_tn(gk_s[:, row_half], n1_half))
    put_attn(2, dot_tn(gv_s[:, row_half], n1_half))
    small_s[0:2, :] = jnp.zeros((2, HALF), f32)
    small_s[6:7, :] = jnp.sum(gq_s[:, row_half].astype(f32), axis=0, keepdims=True)
    small_s[7:8, :] = jnp.sum(gv_s[:, row_half].astype(f32), axis=0, keepdims=True)
    small_s[12:16, :] = jnp.zeros((4, HALF), f32)
    part_ref[...] = mid_s[row_tok, col_half] + og_ref[...]

    for g in range(8):
        down = jnp.concatenate([stage_s[1, 8 * m + g] for m in range(4)], axis=0)
        down = dot_nn(swap, down).astype(bf16)
        attn = jnp.concatenate([stage_s[2, 8 * j + g] for j in range(4)], axis=0)
        attn = dot_nn(swap, attn).astype(bf16)
        for i in range(4):
            to = 4 * g + i
            slot = jnp.bitwise_xor(core, to % 2)
            part = slice(48 * i, 48 * i + 48)
            buf_s[slot, to // 2, 0:48, :] = attn[part]
            buf_s[slot, to // 2, 48:96, :] = stage_s[0, to]
            buf_s[slot, to // 2, 96:144, :] = down[part]
    store_send = pltpu.make_async_copy(buf_s.at[1], send_out, store_sem.at[0])
    store_keep = pltpu.make_async_copy(buf_s.at[0], keep_out, store_sem.at[1])
    store_send.start()
    store_keep.start()
    store_send.wait()
    store_keep.wait()
    store_wqkv.wait()
    store_gqkv.wait()


def input_kernel(
    place_ref, x_ref, vec_ref, gqkv_ref, wqkv_ref, part_ref, some_ref, gin_ref, small_ref, gn1_s, back_s
):
    row_tok = pl.ds(pl.multiple_of(place_ref[0] * 256, 256), 256)
    col_half = pl.ds(pl.multiple_of(place_ref[1] * HALF, 128), HALF)
    for tile in range(2):
        ts = slice(256 * tile, 256 * tile + 256)
        gn1_s[ts, :] = dot_nn(gqkv_ref[ts, :], wqkv_ref[...].reshape(3 * D, D))
    gn1 = gn1_s[...]
    unit1, inverse1 = moments(x_ref[...].astype(f32))
    back_s[...] = norm_back(gn1, unit1, inverse1, vec_ref[0:1, :])
    gin_ref[...] = back_s[row_tok, col_half] + part_ref[...]
    back_s[0:2, :] = jnp.concatenate(
        [jnp.sum(gn1 * unit1, axis=0, keepdims=True), jnp.sum(gn1, axis=0, keepdims=True)], axis=0
    )
    small_ref[...] = some_ref[...]
    small_ref[0:2, :] = back_s[0:2, col_half]


def input_gradient(place, *operands):
    whole = pl.BlockSpec(memory_space=VMEM)
    return pl.pallas_call(
        input_kernel,
        in_specs=[pl.BlockSpec(memory_space=pltpu.SMEM)] + [whole] * len(operands),
        out_specs=[whole] * 2,
        out_shape=[
            jax.ShapeDtypeStruct((256, HALF), f32),
            jax.ShapeDtypeStruct((16, HALF), f32),
        ],
        scratch_shapes=[VMEM((TOK, D), f32), VMEM((TOK, D), f32)],
        compiler_params=pltpu.CompilerParams(vmem_limit_bytes=32 * 1024 * 1024),
        cost_estimate=pl.CostEstimate(
            flops=6 * TOK * D * D, bytes_accessed=8 * 1024 * 1024, transcendentals=0
        ),
        name="input_gradient",
    )(place, *operands)


def layer(place, lengths, *operands):
    smem = pl.BlockSpec(memory_space=pltpu.SMEM)
    whole = pl.BlockSpec(memory_space=VMEM)
    anywhere = pl.BlockSpec(memory_space=pl.ANY)
    return pl.pallas_call(
        layer_kernel,
        in_specs=[smem, smem, anywhere, whole, anywhere, anywhere]
        + [whole] * (len(operands) - 5)
        + [anywhere],
        out_specs=[whole, whole, whole, anywhere, anywhere, anywhere, anywhere],
        out_shape=[
            jax.ShapeDtypeStruct((256, HALF), f32),
            jax.ShapeDtypeStruct((256, HALF), f32),
            jax.ShapeDtypeStruct((16, HALF), f32),
            jax.ShapeDtypeStruct((16, 144, HALF), bf16),
            jax.ShapeDtypeStruct((16, 144, HALF), bf16),
            jax.ShapeDtypeStruct((TOK, 3 * D), bf16),
            jax.ShapeDtypeStruct((3, D, D), bf16),
        ],
        scratch_shapes=[
            pltpu.SemaphoreType.DMA((15,)),
            pltpu.SemaphoreType.DMA((4,)),
            VMEM((TOK, D), bf16),
            VMEM((TOK, D), bf16),
            VMEM((256, HALF), f32),
            VMEM((4, N_DP, 48, HALF), bf16),
            VMEM((3, D, D), bf16),
            VMEM((D, D), bf16),
            VMEM((64, 48, D), bf16),
            VMEM((D, FF), bf16),
            VMEM((2, 16, 144, HALF), bf16),
            VMEM((TOK, TOK), f32),
            VMEM((TOK, D), bf16),
            VMEM((TOK, D), bf16),
            VMEM((TOK, D), bf16),
            VMEM((D, TOK), bf16),
            VMEM((D, TOK), bf16),
            VMEM((12, TOK, TOK), bf16),
            VMEM((D, TOK), bf16),
            VMEM((16, TOK), f32),
            VMEM((TOK, D), bf16),
            VMEM((TOK, D), f32),
            VMEM((TOK, D), bf16),
            VMEM((TOK, FF), bf16),
            VMEM((TOK, FF), bf16),
            VMEM((TOK, D), f32),
            VMEM((D, TOK), bf16),
        ],
        compiler_params=pltpu.CompilerParams(vmem_limit_bytes=60 * 1024 * 1024),
        name="layer",
    )(place, lengths, *operands)


def adam_kernel(data_ref, *refs):
    parts_ref, smalls_ref = refs[0:2]
    masters, firsts, seconds = refs[2:9], refs[9:16], refs[16:23]
    grads, news, updates = refs[23:30], refs[30:37], refs[37:44]
    total = parts_ref[0].astype(f32)
    for i in range(1, 16):
        total = total + parts_ref[i].astype(f32)
    data = data_ref[0]
    lows = jnp.sum(smalls_ref[...], axis=0)
    small = pltpu.roll(lows[0:8], HALF - data * 12, 1)
    wide = jnp.concatenate([lows[8 + m : 9 + m] for m in range(4)], axis=1)
    wide = pltpu.roll(jnp.broadcast_to(wide, (8, FF // 2)), FF // 2 - data * 48, 1)
    gradients = (
        total[0:36].reshape(36, 1, HALF),
        total[36:48].reshape(12, 1, HALF),
        total[48:96],
        jnp.concatenate([total[96 + 12 * m : 108 + 12 * m] for m in range(4)], axis=1).reshape(
            12, 1, 4 * HALF
        ),
        small[0:6, 0:12].reshape(6, 1, 12),
        small[6:8, 0:12].reshape(2, 1, 12),
        wide[0:1, 0:48],
    )
    for i in range(7):
        second_new, updated = adam_update(
            masters[i][...], firsts[i][...], seconds[i][...], gradients[i], step_rates[i]
        )
        grads[i][...] = gradients[i]
        news[i][...] = second_new
        updates[i][...] = updated


def update_masters(data, parts, smalls, masters, firsts, seconds):
    whole = pl.BlockSpec(memory_space=VMEM)
    shapes = [jax.ShapeDtypeStruct(m.shape, f32) for m in masters]
    results = pl.pallas_call(
        adam_kernel,
        in_specs=[pl.BlockSpec(memory_space=pltpu.SMEM)] + [whole] * 23,
        out_specs=[whole] * 21,
        out_shape=shapes * 3,
        compiler_params=pltpu.CompilerParams(vmem_limit_bytes=32 * 1024 * 1024),
        name="update_masters",
    )(data, parts, smalls, *masters, *firsts, *seconds)
    return results[0:7], results[7:14], results[14:21]


def adam_update(master, first_old, second_old, gradient, step_rate):
    first_new = beta_one * first_old + (1.0 - beta_one) * gradient
    second_new = beta_two * second_old + (1.0 - beta_two) * gradient * gradient
    ratio = (
        first_new
        / (1.0 - beta_one**STEP)
        / (jnp.sqrt(second_new / (1.0 - beta_two**STEP)) + adam_eps)
    )
    return (second_new, master - step_rate * (ratio + decay_rate * master))


def on_device(
    block_in,
    out_grad,
    seq_lengths,
    weight_qkv,
    first_qkv,
    second_qkv,
    weight_out,
    first_out,
    second_out,
    weight_up,
    first_up,
    second_up,
    weight_down,
    first_down,
    second_down,
    col_params,
    first_col,
    second_col,
    bias_qv,
    first_qv,
    second_qv,
    bias_up,
    first_bup,
    second_bup,
):
    def flat(qkv, out, up, down, col, qv, bup):
        return (
            qkv.transpose(1, 3, 2, 0).reshape(36, 1, HALF),
            out.transpose(2, 1, 0),
            up.transpose(1, 2, 0).reshape(48, HALF),
            down.transpose(2, 1, 0),
            col,
            qv,
            bup,
        )

    def unflat(qkv, out, up, down, col, qv, bup):
        return (
            qkv.reshape(3, 12, 1, HALF).transpose(3, 0, 2, 1),
            out.transpose(2, 1, 0),
            up.reshape(1, 48, HALF).transpose(2, 0, 1),
            down.transpose(2, 1, 0),
            col,
            qv,
            bup,
        )

    masters = flat(weight_qkv, weight_out, weight_up, weight_down, col_params, bias_qv, bias_up)
    firsts = flat(first_qkv, first_out, first_up, first_down, first_col, first_qv, first_bup)
    seconds = flat(second_qkv, second_out, second_up, second_down, second_col, second_qv, second_bup)
    gathered = lax.all_gather(pack_masters(*masters[:4]), ALL, axis=0, tiled=False)
    gathered = gathered.reshape(N_DP, 4, 144, HALF)

    small = jnp.concatenate(
        [col_params.reshape(72), bias_qv.reshape(24), bias_up.reshape(48), jnp.zeros(240, f32)]
    ).astype(bf16)
    small = jnp.concatenate([small.reshape(1, HALF), jnp.zeros((15, HALF), bf16)], axis=0)
    four = lax.all_gather(
        jnp.concatenate([block_in, small], axis=0), ("row", "col"), axis=0, tiled=False
    )

    def whole_rows(four):
        return four.reshape(2, 2, 256, HALF).transpose(0, 2, 1, 3).reshape(TOK, D)

    rows_full = whole_rows(four[:, 0:256])
    smalls = lax.all_gather(four[:, 256, 0:144], DP, axis=0, tiled=False)
    smalls = smalls.reshape(N_DP, 2, 2, 144).astype(f32)
    vec = smalls[:, 0, :, 0:72].reshape(N_DP, 2, 6, 12).transpose(2, 1, 0, 3).reshape(6, D)
    vec = jnp.concatenate([vec, jnp.zeros((2, D), f32)], axis=0)
    bqv = smalls[:, :, 0, 72:96].reshape(N_DP, 2, 2, 12).transpose(2, 1, 0, 3).reshape(2, D)
    bqkv = jnp.stack([bqv[0], jnp.zeros_like(bqv[0]), bqv[1]])
    bup = smalls[:, :, 0, 96:144].transpose(1, 0, 2).reshape(1, FF)
    grad_full = whole_rows(
        lax.all_gather(out_grad.astype(bf16), ("row", "col"), axis=0, tiled=False)
    )
    unit_one, _ = moments(rows_full.astype(f32))
    normed_one = (unit_one * vec[0:1] + vec[1:2]).astype(bf16)

    place = jnp.stack([lax.axis_index("row"), lax.axis_index("col"), lax.axis_index("core")])
    place = place.astype(jnp.int32)
    result, part, some, keep, send, gqkv, wqkv = layer(
        place,
        seq_lengths,
        rows_full,
        normed_one,
        grad_full,
        out_grad,
        vec,
        bqkv,
        bup,
        swap_matrix(),
        gathered,
    )

    other = lax.ppermute(send, "core", [(0, 1), (1, 0)])
    both = (keep.astype(f32) + other.astype(f32)).astype(bf16)
    both, part = lax.optimization_barrier((both, part))
    parts = lax.all_to_all(both, ("y", "x"), 0, 0, tiled=True)
    grad_in, small = input_gradient(place, rows_full, vec, gqkv, wqkv, part, some)
    smalls = lax.all_gather(small, DP, axis=0, tiled=False)
    data = lax.axis_index(DP).astype(jnp.int32).reshape(1)
    grads, news, updates = update_masters(data, parts, smalls, masters, firsts, seconds)
    outputs = [result, grad_in]
    for triple in zip(unflat(*grads), unflat(*news), unflat(*updates)):
        outputs += triple
    return tuple(outputs)


def solution(mesh):
    fine = Mesh(mesh.devices.reshape(4, 4, 2, 2, 2), ALL)
    qkv_spec = P("col", None, "row", DP)
    out_spec = P("row", "col", DP)
    up_spec = P("col", "row", DP)
    down_spec = P("row", "col", DP)
    col_spec = P(None, "col", DP)
    qv_spec = P(None, "row", DP)
    bup_spec = P("row", DP)
    rows_spec = P(DP + ("row",), "col")
    params = (qkv_spec, out_spec, up_spec, down_spec, col_spec, qv_spec, bup_spec)
    triples = tuple(spec for spec in params for _ in range(3))
    return jax.shard_map(
        on_device,
        mesh=fine,
        in_specs=(rows_spec, rows_spec, P(DP, None)) + triples,
        out_specs=(rows_spec, rows_spec) + triples,
        check_vma=False,
    )
```

```python
import functools

import jax
import jax.numpy as jnp
import numpy as np
from jax import lax
from jax.experimental import pallas as pl
from jax.experimental.pallas import tpu as pltpu
from jax.sharding import Mesh
from jax.sharding import PartitionSpec as P

HD = 64
D = 768
HALF = 384
FF = 3072
TOK = 512
QW = 256
QB = 2
N_DP = 32
STEP = 10

norm_eps = 1e-05
beta_one = 0.9
beta_two = 0.999
adam_eps = 1e-08
decay_rate = 0.1
neg_large = -1e30
step_rates = (0.25, 0.4, 0.25, 0.25, 0.3, 0.3, 0.3)

DP = ("y", "x", "core")
ALL = ("y", "x", "core", "row", "col")
bf16 = jnp.bfloat16
f32 = jnp.float32
VMEM = pltpu.VMEM


def swap_matrix():
    places = np.arange(192).reshape(4, 4, 12).transpose(1, 0, 2).reshape(192)
    return jnp.asarray(np.eye(192, dtype=np.float32)[places], dtype=bf16)


def dot_nn(a, b):
    return lax.dot_general(a, b, (((1,), (0,)), ((), ())), preferred_element_type=f32)


def dot_nt(a, b):
    return lax.dot_general(a, b, (((1,), (1,)), ((), ())), preferred_element_type=f32)


def dot_tn(a, b):
    return lax.dot_general(a, b, (((0,), (0,)), ((), ())), preferred_element_type=f32)


def masters_kernel(qkv_ref, out_ref, up_ref, down_ref, shard_ref):
    shard_ref[0:48, :] = jnp.concatenate([qkv_ref[:, 0, :], out_ref[:, 0, :]], axis=0).astype(bf16)
    shard_ref[48:96, :] = up_ref[...].astype(bf16)
    shard_ref[96:144, :] = jnp.concatenate(
        [down_ref[:, 0, HALF * m : HALF * m + HALF] for m in range(4)], axis=0
    ).astype(bf16)


def pack_masters(qkv, out, up, down):
    whole = pl.BlockSpec(memory_space=VMEM)
    return pl.pallas_call(
        masters_kernel,
        in_specs=[whole] * 4,
        out_specs=whole,
        out_shape=jax.ShapeDtypeStruct((144, HALF), bf16),
        name="pack_masters",
    )(qkv, out, up, down)


def moments(values):
    mean = jnp.sum(values, axis=1, keepdims=True) * (1.0 / D)
    centered = values - mean
    spread = jnp.sum(centered * centered, axis=1, keepdims=True) * (1.0 / D)
    inverse = lax.rsqrt(spread + norm_eps)
    return centered * inverse, inverse


def norm_back(grad_norm, unit, inverse, gain):
    scaled = grad_norm * gain
    total = jnp.sum(scaled, axis=1, keepdims=True) * (1.0 / D)
    crossed = jnp.sum(scaled * unit, axis=1, keepdims=True) * (1.0 / D)
    return inverse * (scaled - total - unit * crossed)


def gelu_pair(x):
    c = 0.7978845608028654
    square = x * x
    t = jnp.tanh(x * (c + (0.044715 * c) * square))
    half = 0.5 + 0.5 * t
    value = x * half
    slope = half + value * (1.0 - t) * (c + (3.0 * 0.044715 * c) * square)
    return value, slope


def layer_kernel(
    place_ref,
    lengths_ref,
    x_hbm,
    n1_ref,
    gl_hbm,
    og_hbm,
    vec_ref,
    bqkv_ref,
    bup_ref,
    swap_ref,
    gathered_ref,
    result_ref,
    gin_ref,
    keep_out,
    send_out,
    load_sem,
    store_sem,
    x_ref,
    gl_ref,
    og_ref,
    stage_s,
    wqkv_s,
    wout_s,
    wup_s,
    wdown_s,
    small_s,
    early_s,
    late_s,
    bias_s,
    q_s,
    k_s,
    v_s,
    vt_s,
    kt_s,
    p_s,
    at_s,
    share_s,
    a_s,
    mid_s,
    n2_s,
    act_s,
    gh_s,
    gn2_s,
    gqt_s,
):
    row = place_ref[0]
    col = place_ref[1]
    row_tok = pl.ds(pl.multiple_of(row * 256, 256), 256)
    row_half = pl.ds(pl.multiple_of(row * HALF, 128), HALF)
    col_half = pl.ds(pl.multiple_of(col * HALF, 128), HALF)

    core = place_ref[2]
    swap = swap_ref[...]
    load_attn = [
        pltpu.make_async_copy(gathered_ref.at[:, s, 0:48, :], stage_s.at[s], load_sem.at[s])
        for s in range(4)
    ]
    load_up = [
        pltpu.make_async_copy(
            gathered_ref.at[:, s, 48:96, :],
            wup_s.at[32 * (s // 2) : 32 * (s // 2) + 32, :, HALF * (s % 2) : HALF * (s % 2) + HALF],
            load_sem.at[4 + s],
        )
        for s in range(4)
    ]
    load_down = [
        pltpu.make_async_copy(gathered_ref.at[:, s, 96:144, :], stage_s.at[s], load_sem.at[8 + s])
        for s in range(4)
    ]
    load_rows = [
        pltpu.make_async_copy(source, target, load_sem.at[12 + i])
        for i, (source, target) in enumerate(((x_hbm, x_ref), (gl_hbm, gl_ref), (og_hbm, og_ref)))
    ]
    for copy in load_attn + load_rows:
        copy.start()

    def unswapped(s, g):
        block = stage_s[s, 4 * g : 4 * g + 4].reshape(192, HALF)
        return dot_nn(swap, block).astype(bf16)

    e0 = lengths_ref[0, 0]
    e1 = e0 + lengths_ref[0, 1]
    e2 = e1 + lengths_ref[0, 2]
    key_place = lax.broadcasted_iota(jnp.int32, (TOK, 1), 0)
    query_place = lax.broadcasted_iota(jnp.int32, (1, TOK), 1)

    def segment(places):
        return (
            (places >= e0).astype(jnp.int32)
            + (places >= e1).astype(jnp.int32)
            + (places >= e2).astype(jnp.int32)
        )

    allowed = (segment(key_place) == segment(query_place)) & (key_place <= query_place)
    bias_s[...] = jnp.where(allowed, 0.0, neg_large)

    for s in range(4):
        load_attn[s].wait()
        outer = HALF * (s // 2)
        inner = HALF * (s % 2)
        for g in range(8):
            block = unswapped(s, g)
            for j in range(3):
                wqkv_s[j, outer + 48 * g : outer + 48 * g + 48, inner : inner + HALF] = block[
                    48 * j : 48 * j + 48
                ]
            wout_s[inner + 48 * g : inner + 48 * g + 48, outer : outer + HALF] = block[144:192]
        load_up[s].start()
        load_down[s].start()

    n1 = n1_ref[...]
    queries = (dot_nt(n1, wqkv_s[0]) + bqkv_ref[0:1, :]).astype(bf16)
    q_s[...] = queries * jnp.asarray(HD**-0.5, bf16)
    keys = dot_nt(n1, wqkv_s[1]).astype(bf16)
    k_s[...] = keys
    kt_s[...] = keys.T
    values = (dot_nt(n1, wqkv_s[2]) + bqkv_ref[2:3, :]).astype(bf16)
    v_s[...] = values
    vt_s[...] = values.T

    lane = lax.broadcasted_iota(jnp.int32, (1, 128), 1)

    for pair in range(6):
        lanes = slice(pair * 128, pair * 128 + 128)
        q_pair = q_s[:, lanes]
        k_pair = k_s[:, lanes]
        for hh in range(2):
            mine = (lane < HD) if hh == 0 else (lane >= HD)
            q_one = jnp.where(mine, q_pair, jnp.zeros_like(q_pair))
            rows = slice(pair * 128 + hh * HD, pair * 128 + hh * HD + HD)
            for j in range(QB):
                kn = QW * (j + 1)
                qs = slice(QW * j, QW * j + QW)
                scores = dot_nt(k_pair[:kn], q_one[qs]) + bias_s[:kn, qs]
                top = jnp.max(scores, axis=0, keepdims=True)
                weights = jnp.exp(scores - top)
                share = 1.0 / jnp.sum(weights, axis=0, keepdims=True)
                weights = weights.astype(bf16)
                p_s[2 * pair + hh, :kn, qs] = weights
                share_s[2 * pair + hh : 2 * pair + hh + 1, qs] = share
                at_s[rows, qs] = (dot_nn(vt_s[rows, :kn], weights) * share).astype(bf16)

    a_s[...] = at_s[...].T
    share_t = share_s[...].T

    for copy in load_rows:
        copy.wait()
    mid = x_ref[...].astype(f32) + dot_nt(a_s[...], wout_s[...]) + vec_ref[4:5, :]
    mid_s[...] = mid
    unit2, inverse2 = moments(mid)
    n2_s[...] = (unit2 * vec_ref[2:3, :] + vec_ref[3:4, :]).astype(bf16)

    for s in range(4):
        load_up[s].wait()
        load_down[s].wait()
        outer = HALF * (s % 2)
        inner = (FF // 2) * (s // 2)
        for g in range(8):
            block = unswapped(s, g)
            for m in range(4):
                wdown_s[
                    outer + 48 * g : outer + 48 * g + 48, inner + HALF * m : inner + HALF * m + HALF
                ] = block[48 * m : 48 * m + 48]
    for chunk in range(4):
        units = slice(D * chunk, D * chunk + D)
        up = wup_s[16 * chunk : 16 * chunk + 16].reshape(D, D)
        for tile in range(2):
            ts = slice(256 * tile, 256 * tile + 256)
            hidden = dot_nt(n2_s[ts, :], up) + bup_ref[:, units]
            value, slope = gelu_pair(hidden)
            act_s[ts, units] = value.astype(bf16)
            grad_act = dot_nn(gl_ref[ts, :], wdown_s[:, units])
            grad_hidden = (grad_act * slope).astype(bf16)
            gh_s[ts, units] = grad_hidden
    for tile in range(2):
        ts = slice(256 * tile, 256 * tile + 256)
        gn2_s[ts, :] = dot_nn(gh_s[ts, :], wup_s[...].reshape(FF, D))
    result_ref[...] = (
        mid_s[row_tok, col_half]
        + vec_ref[5:6, col_half]
        + dot_nt(act_s[row_tok, :], wdown_s[col_half, :])
    )
    row_units = pl.ds(pl.multiple_of(row * (FF // 2), 128), FF // 2)
    grad_up = dot_tn(gh_s[:, row_units], n2_s[:, col_half]).astype(bf16)
    stage_s[0] = grad_up.reshape(N_DP, 48, HALF)
    for m in range(4):
        quarter = pl.ds(pl.multiple_of(row * (FF // 2) + HALF * m, 128), HALF)
        grad_down = dot_tn(gl_ref[:, col_half], act_s[:, quarter]).astype(bf16)
        stage_s[1, 8 * m : 8 * m + 8] = grad_down.reshape(8, 48, HALF)
    sums = jnp.sum(gh_s[:, row_units].astype(f32), axis=0, keepdims=True)
    for part in range(4):
        small_s[8 + part : 9 + part, :] = sums[:, HALF * part : HALF * part + HALF]

    for g in range(8):
        down = jnp.concatenate([stage_s[1, 8 * m + g] for m in range(4)], axis=0)
        down = dot_nn(swap, down).astype(bf16)
        for i in range(4):
            to = 4 * g + i
            slot = jnp.bitwise_xor(core, to % 2)
            early_s[slot, to // 2, 0:48, :] = stage_s[0, to]
            early_s[slot, to // 2, 48:96, :] = down[48 * i : 48 * i + 48]

    def stores(source, rows, first):
        return [
            pltpu.make_async_copy(source.at[1 - i], target.at[:, rows, :], store_sem.at[first + i])
            for i, target in enumerate((send_out, keep_out))
        ]

    store_early = stores(early_s, slice(0, 96), 0)
    for copy in store_early:
        copy.start()

    ga_s = gh_s.at[:, 0:D]
    gq_s = gh_s.at[:, D : 2 * D]
    gk_s = gh_s.at[:, 2 * D : 3 * D]
    gv_s = gh_s.at[:, 3 * D : 4 * D]
    gm_s = act_s.at[:, 0:D]
    gn2 = gn2_s[...]
    unit2, inverse2 = moments(mid_s[...])
    delta = norm_back(gn2, unit2, inverse2, vec_ref[2:3, :])
    grad_mid = delta + gl_ref[...].astype(f32)
    gm_s[...] = grad_mid.astype(bf16)
    mid_s[...] = delta


    sums_rows = jnp.concatenate(
        [
            jnp.sum(gn2 * unit2, axis=0, keepdims=True),
            jnp.sum(gn2, axis=0, keepdims=True),
            jnp.sum(grad_mid, axis=0, keepdims=True),
            jnp.sum(gl_ref[...].astype(f32), axis=0, keepdims=True),
        ],
        axis=0,
    )
    gn2_s[0:4, :] = sums_rows
    small_s[2:6, :] = gn2_s[0:4, col_half]
    ga_s[...] = dot_nn(gm_s[...], wout_s[...]).astype(bf16)

    def put_attn(j, grad):
        stage_s[2, 8 * j : 8 * j + 8] = grad.astype(bf16).reshape(8, 48, HALF)

    put_attn(3, dot_tn(gm_s[:, col_half], a_s[:, row_half]))

    for pair in range(6):
        lanes = slice(pair * 128, pair * 128 + 128)
        q_pair = q_s[:, lanes]
        v_pair = v_s[:, lanes]
        g_pair = ga_s[:, lanes]
        grad_keys = []
        grad_values = []
        for hh in range(2):
            mine = (lane < HD) if hh == 0 else (lane >= HD)
            head = 2 * pair + hh
            g_all = (g_pair.astype(f32) * share_t[:, head : head + 1]).astype(bf16)
            g_one = jnp.where(mine, g_all, jnp.zeros_like(g_all))
            rows = slice(pair * 128 + hh * HD, pair * 128 + hh * HD + HD)
            gk_parts = []
            gv_parts = []
            for j in range(2):
                kn = 256 * (j + 1)
                qs = slice(256 * j, 256 * j + 256)
                weights_low = p_s[head, :kn, qs]
                weights = weights_low.astype(f32)
                grad_probs = dot_nt(v_pair[:kn], g_one[qs])
                inner = jnp.sum(weights * grad_probs, axis=0, keepdims=True)
                inner = inner * share_s[head : head + 1, qs]
                grad_scores = (weights * (grad_probs - inner)).astype(bf16)
                gv_parts.append(dot_nn(weights_low, g_all[qs]))
                gk_parts.append(dot_nn(grad_scores, q_pair[qs]))
                gqt_s[rows, qs] = (dot_nn(kt_s[rows, :kn], grad_scores) * HD**-0.5).astype(bf16)
            grad_keys.append((gk_parts[0] + gk_parts[1][:256], gk_parts[1][256:]))
            grad_values.append((gv_parts[0] + gv_parts[1][:256], gv_parts[1][256:]))
        for piece in range(2):
            ts = slice(256 * piece, 256 * piece + 256)
            gk_s[ts, lanes] = jnp.where(
                lane < HD, grad_keys[0][piece], grad_keys[1][piece]
            ).astype(bf16)
            gv_s[ts, lanes] = jnp.where(
                lane < HD, grad_values[0][piece], grad_values[1][piece]
            ).astype(bf16)

    gq_s[...] = gqt_s[...].T

    n1_half = n1_ref[:, col_half]
    row_rows = pl.ds(pl.multiple_of(row * HALF, HALF), HALF)
    put_attn(0, dot_nn(gqt_s[row_rows, :], n1_half))
    put_attn(1, dot_tn(gk_s[:, row_half], n1_half))
    put_attn(2, dot_tn(gv_s[:, row_half], n1_half))
    small_s[6:7, :] = jnp.sum(gq_s[:, row_half].astype(f32), axis=0, keepdims=True)
    small_s[7:8, :] = jnp.sum(gv_s[:, row_half].astype(f32), axis=0, keepdims=True)
    for tile in range(2):
        ts = slice(256 * tile, 256 * tile + 256)
        gn2_s[ts, :] = dot_nn(gh_s[ts, D : 4 * D], wqkv_s[...].reshape(3 * D, D))
    gn1 = gn2_s[...]
    unit1, inverse1 = moments(x_ref[...].astype(f32))
    mid_s[...] += norm_back(gn1, unit1, inverse1, vec_ref[0:1, :])
    gn2_s[0:2, :] = jnp.concatenate(
        [jnp.sum(gn1 * unit1, axis=0, keepdims=True), jnp.sum(gn1, axis=0, keepdims=True)], axis=0
    )
    small_s[0:2, :] = gn2_s[0:2, col_half]
    small_s[12:16, :] = jnp.zeros((4, HALF), f32)
    gin_ref[...] = mid_s[row_tok, col_half] + og_ref[...]

    put_small = small_s[...].astype(bf16)
    for g in range(8):
        attn = jnp.concatenate([stage_s[2, 8 * j + g] for j in range(4)], axis=0)
        attn = dot_nn(swap, attn).astype(bf16)
        for i in range(4):
            to = 4 * g + i
            slot = jnp.bitwise_xor(core, to % 2)
            late_s[slot, to // 2, 0:48, :] = attn[48 * i : 48 * i + 48]
            late_s[slot, to // 2, 48:64, :] = put_small
    store_late = stores(late_s, slice(96, 160), 2)
    for copy in store_late:
        copy.start()
    for copy in store_early + store_late:
        copy.wait()


def layer(place, lengths, *operands):
    smem = pl.BlockSpec(memory_space=pltpu.SMEM)
    whole = pl.BlockSpec(memory_space=VMEM)
    anywhere = pl.BlockSpec(memory_space=pl.ANY)
    return pl.pallas_call(
        layer_kernel,
        in_specs=[smem, smem, anywhere, whole, anywhere, anywhere]
        + [whole] * (len(operands) - 5)
        + [anywhere],
        out_specs=[whole, whole, anywhere, anywhere],
        out_shape=[
            jax.ShapeDtypeStruct((256, HALF), f32),
            jax.ShapeDtypeStruct((256, HALF), f32),
            jax.ShapeDtypeStruct((16, 160, HALF), bf16),
            jax.ShapeDtypeStruct((16, 160, HALF), bf16),
        ],
        scratch_shapes=[
            pltpu.SemaphoreType.DMA((15,)),
            pltpu.SemaphoreType.DMA((4,)),
            VMEM((TOK, D), bf16),
            VMEM((TOK, D), bf16),
            VMEM((256, HALF), f32),
            VMEM((4, N_DP, 48, HALF), bf16),
            VMEM((3, D, D), bf16),
            VMEM((D, D), bf16),
            VMEM((64, 48, D), bf16),
            VMEM((D, FF), bf16),
            VMEM((16, HALF), f32),
            VMEM((2, 16, 96, HALF), bf16),
            VMEM((2, 16, 64, HALF), bf16),
            VMEM((TOK, TOK), f32),
            VMEM((TOK, D), bf16),
            VMEM((TOK, D), bf16),
            VMEM((TOK, D), bf16),
            VMEM((D, TOK), bf16),
            VMEM((D, TOK), bf16),
            VMEM((12, TOK, TOK), bf16),
            VMEM((D, TOK), bf16),
            VMEM((16, TOK), f32),
            VMEM((TOK, D), bf16),
            VMEM((TOK, D), f32),
            VMEM((TOK, D), bf16),
            VMEM((TOK, FF), bf16),
            VMEM((TOK, FF), bf16),
            VMEM((TOK, D), f32),
            VMEM((D, TOK), bf16),
        ],
        compiler_params=pltpu.CompilerParams(vmem_limit_bytes=60 * 1024 * 1024),
        name="layer",
    )(place, lengths, *operands)


def adam_kernel(data_ref, *refs):
    parts_ref = refs[0]
    masters, firsts, seconds = refs[1:8], refs[8:15], refs[15:22]
    grads, news, updates = refs[22:29], refs[29:36], refs[36:43]
    total = parts_ref[0].astype(f32)
    for i in range(1, 16):
        total = total + parts_ref[i].astype(f32)
    data = data_ref[0]
    small = pltpu.roll(total[144:152], HALF - data * 12, 1)
    wide = jnp.concatenate([total[152 + m : 153 + m] for m in range(4)], axis=1)
    wide = pltpu.roll(jnp.broadcast_to(wide, (8, FF // 2)), FF // 2 - data * 48, 1)
    gradients = (
        total[96:132].reshape(36, 1, HALF),
        total[132:144].reshape(12, 1, HALF),
        total[0:48],
        jnp.concatenate([total[48 + 12 * m : 60 + 12 * m] for m in range(4)], axis=1).reshape(
            12, 1, 4 * HALF
        ),
        small[0:6, 0:12].reshape(6, 1, 12),
        small[6:8, 0:12].reshape(2, 1, 12),
        wide[0:1, 0:48],
    )
    for i in range(7):
        second_new, updated = adam_update(
            masters[i][...], firsts[i][...], seconds[i][...], gradients[i], step_rates[i]
        )
        grads[i][...] = gradients[i]
        news[i][...] = second_new
        updates[i][...] = updated


def update_masters(data, parts, masters, firsts, seconds):
    whole = pl.BlockSpec(memory_space=VMEM)
    shapes = [jax.ShapeDtypeStruct(m.shape, f32) for m in masters]
    results = pl.pallas_call(
        adam_kernel,
        in_specs=[pl.BlockSpec(memory_space=pltpu.SMEM)] + [whole] * 22,
        out_specs=[whole] * 21,
        out_shape=shapes * 3,
        compiler_params=pltpu.CompilerParams(vmem_limit_bytes=32 * 1024 * 1024),
        name="update_masters",
    )(data, parts, *masters, *firsts, *seconds)
    return results[0:7], results[7:14], results[14:21]


def adam_update(master, first_old, second_old, gradient, step_rate):
    first_new = beta_one * first_old + (1.0 - beta_one) * gradient
    second_new = beta_two * second_old + (1.0 - beta_two) * gradient * gradient
    ratio = (
        first_new
        / (1.0 - beta_one**STEP)
        / (jnp.sqrt(second_new / (1.0 - beta_two**STEP)) + adam_eps)
    )
    return (second_new, master - step_rate * (ratio + decay_rate * master))


def on_device(
    block_in,
    out_grad,
    seq_lengths,
    weight_qkv,
    first_qkv,
    second_qkv,
    weight_out,
    first_out,
    second_out,
    weight_up,
    first_up,
    second_up,
    weight_down,
    first_down,
    second_down,
    col_params,
    first_col,
    second_col,
    bias_qv,
    first_qv,
    second_qv,
    bias_up,
    first_bup,
    second_bup,
):
    def flat(qkv, out, up, down, col, qv, bup):
        return (
            qkv.transpose(1, 3, 2, 0).reshape(36, 1, HALF),
            out.transpose(2, 1, 0),
            up.transpose(1, 2, 0).reshape(48, HALF),
            down.transpose(2, 1, 0),
            col,
            qv,
            bup,
        )

    def unflat(qkv, out, up, down, col, qv, bup):
        return (
            qkv.reshape(3, 12, 1, HALF).transpose(3, 0, 2, 1),
            out.transpose(2, 1, 0),
            up.reshape(1, 48, HALF).transpose(2, 0, 1),
            down.transpose(2, 1, 0),
            col,
            qv,
            bup,
        )

    masters = flat(weight_qkv, weight_out, weight_up, weight_down, col_params, bias_qv, bias_up)
    firsts = flat(first_qkv, first_out, first_up, first_down, first_col, first_qv, first_bup)
    seconds = flat(second_qkv, second_out, second_up, second_down, second_col, second_qv, second_bup)
    gathered = lax.all_gather(pack_masters(*masters[:4]), ALL, axis=0, tiled=False)
    gathered = gathered.reshape(N_DP, 4, 144, HALF)

    small = jnp.concatenate(
        [col_params.reshape(72), bias_qv.reshape(24), bias_up.reshape(48), jnp.zeros(240, f32)]
    ).astype(bf16)
    small = jnp.concatenate([small.reshape(1, HALF), jnp.zeros((15, HALF), bf16)], axis=0)
    four = lax.all_gather(
        jnp.concatenate([block_in, small], axis=0), ("row", "col"), axis=0, tiled=False
    )

    def whole_rows(four):
        return four.reshape(2, 2, 256, HALF).transpose(0, 2, 1, 3).reshape(TOK, D)

    rows_full = whole_rows(four[:, 0:256])
    smalls = lax.all_gather(four[:, 256, 0:144], DP, axis=0, tiled=False)
    smalls = smalls.reshape(N_DP, 2, 2, 144).astype(f32)
    vec = smalls[:, 0, :, 0:72].reshape(N_DP, 2, 6, 12).transpose(2, 1, 0, 3).reshape(6, D)
    vec = jnp.concatenate([vec, jnp.zeros((2, D), f32)], axis=0)
    bqv = smalls[:, :, 0, 72:96].reshape(N_DP, 2, 2, 12).transpose(2, 1, 0, 3).reshape(2, D)
    bqkv = jnp.stack([bqv[0], jnp.zeros_like(bqv[0]), bqv[1]])
    bup = smalls[:, :, 0, 96:144].transpose(1, 0, 2).reshape(1, FF)
    grad_full = whole_rows(
        lax.all_gather(out_grad.astype(bf16), ("row", "col"), axis=0, tiled=False)
    )
    unit_one, _ = moments(rows_full.astype(f32))
    normed_one = (unit_one * vec[0:1] + vec[1:2]).astype(bf16)

    place = jnp.stack([lax.axis_index("row"), lax.axis_index("col"), lax.axis_index("core")])
    result, grad_in, keep, send = layer(
        place.astype(jnp.int32),
        seq_lengths,
        rows_full,
        normed_one,
        grad_full,
        out_grad,
        vec,
        bqkv,
        bup,
        swap_matrix(),
        gathered,
    )

    other = lax.ppermute(send, "core", [(0, 1), (1, 0)])
    both = (keep.astype(f32) + other.astype(f32)).astype(bf16)
    parts = lax.all_to_all(both, ("y", "x"), 0, 0, tiled=True)
    data = lax.axis_index(DP).astype(jnp.int32).reshape(1)
    grads, news, updates = update_masters(data, parts, masters, firsts, seconds)
    outputs = [result, grad_in]
    for triple in zip(unflat(*grads), unflat(*news), unflat(*updates)):
        outputs += triple
    return tuple(outputs)


def solution(mesh):
    fine = Mesh(mesh.devices.reshape(4, 4, 2, 2, 2), ALL)
    qkv_spec = P("col", None, "row", DP)
    out_spec = P("row", "col", DP)
    up_spec = P("col", "row", DP)
    down_spec = P("row", "col", DP)
    col_spec = P(None, "col", DP)
    qv_spec = P(None, "row", DP)
    bup_spec = P("row", DP)
    rows_spec = P(DP + ("row",), "col")
    params = (qkv_spec, out_spec, up_spec, down_spec, col_spec, qv_spec, bup_spec)
    triples = tuple(spec for spec in params for _ in range(3))
    return jax.shard_map(
        on_device,
        mesh=fine,
        in_specs=(rows_spec, rows_spec, P(DP, None)) + triples,
        out_specs=(rows_spec, rows_spec) + triples,
        check_vma=False,
    )
```
